32 devices in a mesh: seq: 8 (over z, x), mp: 4 (over y, core).
Axes of the slice: x: 2, y: 2, z: 4, core: 2. Of those that a mesh axis runs over, the one named last changes fastest.
Arguments:
- hidden: bfloat16 [2048, 4096], P('seq', 'mp'), may hold values from -6 to 6
- cotangent: bfloat16 [2048, 4096], P('seq', 'mp'), may hold values from -6 to 6
- neighbour_ids: int32 [32, 2, 128], P('seq'), may hold values from 0 to 63999
- neighbour_lengths: int32 [32, 2], replicated, may hold values from 1 to 128
- embed_table: bfloat16 [64000, 896], P('mp'), may hold values from -6 to 6
- enc_up: bfloat16 [3584, 896], P('mp'), may hold values from -0.1875 to 0.1875
- enc_down: bfloat16 [3584, 896], P('mp'), may hold values from -0.09375 to 0.09375
- w_query: bfloat16 [4096, 32, 128], P('seq', 'mp'), may hold values from -0.125 to 0.125
- w_keyval: bfloat16 [896, 32, 2, 128], P('seq', 'mp'), may hold values from -0.1875 to 0.1875
- w_out: bfloat16 [4096, 32, 128], P('seq', 'mp'), may hold values from -0.75 to 0.75
Outputs:
- cca_out: bfloat16 [2048, 4096], P('seq', 'mp')
- hidden_grad: bfloat16 [2048, 4096], P('seq', 'mp')
The draws below stay inside these ranges and needn't reach their ends.
All inputs are finite; a program needn't handle non-finite values.
Results may differ from the reference program's by a relative error of at most 0.012.
Values may be sent and summed in bfloat16 or wider, within the bound.
No kernel may reach another device: no remote copies, remote signals or barrier semaphores. Data moves between devices by JAX's collectives and lax.ppermute only.
A program may use at most 128 MiB of HBM per device.

```python
import math
import jax
import jax.numpy as jnp
import numpy as np
from jax import lax

D = 4096
HEADS = 32
HD = 128
ENC = 896
ENC_FF = 3584
VOCAB = 64000
SPAN = 64
NEIGH = 2
NLEN = 128
SPANS = 32
SEQ_LEN = 2048


def place_ends(drawn, rng, least, top_value):
    spot = [jax.random.randint(jax.random.fold_in(rng, axis), (), 0, length) for axis, length in enumerate(drawn.shape)]
    widest = drawn.shape.index(max(drawn.shape))
    next_to = spot[:widest] + [(spot[widest] + 1) % drawn.shape[widest]] + spot[widest + 1:]
    return drawn.at[tuple(spot)].set(least).at[tuple(next_to)].set(top_value)


def spiked(entries, own_key, source, target, blocks, factor):
    owner, partner = [(jnp.arange(entries.shape[dim]) // (entries.shape[dim] // blocks)).reshape([-1 if axis == dim else 1 for axis in range(entries.ndim)]) for dim in (source, target)]
    chosen = jax.random.permutation(own_key, blocks)[partner]
    strong = (owner == chosen) | (owner == (partner + blocks // 2) % blocks)
    return jnp.where(strong, factor * entries, entries)


def block_scale(stream_key, extent, pieces, smallest, top_value):
    def one(position, shards_of):
        heights = jax.random.uniform(jax.random.fold_in(jax.random.fold_in(stream_key, 6), position), (shards_of,), jnp.float32, smallest / len(pieces), top_value / len(pieces))
        return jnp.repeat(jnp.exp(heights), extent[position] // shards_of).reshape((-1,) + (1,) * (len(extent) - position - 1))

    gain = one(*pieces[0])
    for cut in pieces[1:]:
        gain = gain * one(*cut)
    return gain


def cumulative_ranks(number_of, skew):
    portions = [(1 << 20) // math.isqrt(rank ** skew) + 1 for rank in range(1, number_of + 1)]
    deviation = 1 + sum(portions) // (1 << 30)
    return np.cumsum(np.array([max(1, weight // deviation) for weight in portions]))


def skewed_ids(own_key, shape, count, lean):
    table = cumulative_ranks(count, lean)
    pick = jax.random.randint(jax.random.fold_in(own_key, 1), shape, 0, int(table[count - 1]))
    grade = jnp.searchsorted(jnp.asarray(table, jnp.int32), pick, side="right")
    return jax.random.permutation(jax.random.fold_in(own_key, 2), count)[grade].astype(jnp.int32)


def normal_values(own_key, dims, spread, reach, pieces=(), kind=jnp.bfloat16):
    level = block_scale(own_key, dims, pieces, -0.22, 0.18) if pieces else 1.0
    result = jax.random.normal(own_key, dims, jnp.float32) * spread * level
    return jnp.minimum(jnp.maximum(result, -reach), reach).astype(kind)


def bell_draw_with(key, dims, scale, bound, shards, heavy, kind=jnp.bfloat16):
    entries = scale * jax.random.normal(key, dims, jnp.float32)
    if shards:
        entries = entries * block_scale(key, dims, shards, -0.22, 0.18)
    return jnp.clip(spiked(entries, jax.random.fold_in(key, 3), *heavy), -bound, bound).astype(kind)


def setup_inputs(seed: int = 0) -> dict:
    splits = jax.random.split(jax.random.key(seed), 11)
    return {
        "hidden": normal_values(splits[0], (SEQ_LEN, D), 1.0, 6.0, ((0, 8), (1, 4))),
        "cotangent": normal_values(splits[1], (SEQ_LEN, D), 1.0, 6.0, ((0, 8), (1, 4))),
        "neighbour_ids": place_ends(skewed_ids(splits[2], (SPANS, NEIGH, NLEN), VOCAB, 2), jax.random.fold_in(splits[2], 3), 0, VOCAB - 1).astype(jnp.int32),
        "neighbour_lengths": place_ends(jax.random.randint(splits[3], (SPANS, NEIGH), 1, NLEN + 1), jax.random.fold_in(splits[3], 1), 1, NLEN).astype(jnp.int32),
        "embed_table": normal_values(splits[4], (VOCAB, ENC), 1.0, 6.0, ((0, 4),)),
        "enc_up": normal_values(splits[5], (ENC_FF, ENC), ENC ** -0.5, 0.1875, ((0, 4),)),
        "enc_down": normal_values(splits[6], (ENC_FF, ENC), ENC_FF ** -0.5, 0.09375, ((0, 4),)),
        "w_query": bell_draw_with(splits[7], (D, HEADS, HD), D ** -0.5, 0.125, ((0, 8), (1, 4)), (1, 0, 8, 2.0)),
        "w_keyval": normal_values(splits[8], (ENC, HEADS, 2, HD), ENC ** -0.5, 0.1875, ((0, 8), (1, 4))),
        "w_out": bell_draw_with(splits[9], (D, HEADS, HD), HD ** -0.5, 0.75, ((0, 8), (1, 4)), (1, 0, 8, 2.0)),
    }


def rms_rows(values):
    return values * lax.rsqrt(lax.optimization_barrier(jnp.mean(values * values, axis=-1, keepdims=True)) + 1e-06)

def shift_rows(flat):
    width = flat.shape[1]
    front = jnp.zeros((1, width), flat.dtype)
    back = jnp.zeros((SPAN - 1, width), flat.dtype)
    return jnp.concatenate([front, flat, back], axis=0)

def reference(hidden, cotangent, neighbour_ids, neighbour_lengths, embed_table, enc_up, enc_down, w_query, w_keyval, w_out):
    groups = SPANS + 1
    keys_per = NEIGH * NLEN
    inner = HEADS * HD
    scale = HD ** (-0.5)
    emb = jnp.take(embed_table, neighbour_ids.reshape(SPANS * keys_per), axis=0)
    emb_wide = emb.astype(jnp.float32)
    normed = rms_rows(emb_wide).astype(jnp.bfloat16)
    act = jax.nn.gelu(jnp.dot(normed, enc_up.T, preferred_element_type=jnp.float32)).astype(jnp.bfloat16)
    ffn = jnp.dot(act, enc_down, preferred_element_type=jnp.float32)
    encoded = rms_rows(emb_wide + ffn).astype(jnp.bfloat16)
    keyval = jnp.dot(encoded, w_keyval.reshape(ENC, 2 * inner), preferred_element_type=jnp.float32).astype(jnp.bfloat16)
    keyval = keyval.reshape(SPANS, keys_per, HEADS, 2, HD)
    empty = jnp.zeros((1, keys_per, HEADS, 2, HD), jnp.bfloat16)
    keyval = jnp.concatenate([empty, keyval], axis=0)
    keys = keyval[:, :, :, 0].astype(jnp.float32)
    values = keyval[:, :, :, 1].astype(jnp.float32)
    lens = jnp.concatenate([jnp.ones((1, NEIGH), jnp.int32), neighbour_lengths], axis=0)
    key_mask = (jnp.arange(NLEN, dtype=jnp.int32)[None, None, :] < lens[:, :, None]).reshape(groups, keys_per)
    valid = (jnp.arange(groups) > 0).astype(jnp.float32)
    wq_flat = w_query.reshape(D, inner)
    wo_flat = w_out.reshape(D, inner)
    query = jnp.dot(hidden, wq_flat, preferred_element_type=jnp.float32).astype(jnp.bfloat16)
    query_g = shift_rows(query).reshape(groups, SPAN, HEADS, HD).astype(jnp.float32)
    scores = jnp.einsum('gqhd,gkhd->ghqk', query_g, keys) * scale
    expo = jnp.where(key_mask[:, None, None, :], jnp.exp(scores), 0.0)
    prob = expo / lax.optimization_barrier(jnp.sum(expo, axis=-1, keepdims=True)) * valid[:, None, None, None]
    prob_low = prob.astype(jnp.bfloat16).astype(jnp.float32)
    attn = jnp.einsum('ghqk,gkhd->gqhd', prob_low, values).astype(jnp.bfloat16)
    attn_flat = attn.reshape(groups * SPAN, inner)[1:SEQ_LEN + 1]
    cca_out = jnp.dot(attn_flat, wo_flat.T, preferred_element_type=jnp.float32).astype(jnp.bfloat16)
    d_attn = jnp.dot(cotangent, wo_flat, preferred_element_type=jnp.float32).astype(jnp.bfloat16)
    d_group = shift_rows(d_attn).reshape(groups, SPAN, HEADS, HD).astype(jnp.float32)
    d_prob = jnp.einsum('gqhd,gkhd->ghqk', d_group, values)
    delta = lax.optimization_barrier(jnp.sum(prob * d_prob, axis=-1, keepdims=True))
    d_score = (prob * (d_prob - delta) * scale).astype(jnp.bfloat16).astype(jnp.float32)
    d_query = jnp.einsum('ghqk,gkhd->gqhd', d_score, keys).astype(jnp.bfloat16)
    d_flat = d_query.reshape(groups * SPAN, inner)[1:SEQ_LEN + 1]
    hidden_grad = jnp.dot(d_flat, wq_flat.T, preferred_element_type=jnp.float32).astype(jnp.bfloat16)
    return (cca_out, hidden_grad)
```

```python
import functools

import jax
import jax.numpy as jnp
from jax import lax
from jax.experimental import pallas as pl
from jax.experimental.pallas import tpu as pltpu
from jax.sharding import Mesh
from jax.sharding import PartitionSpec as P

SEQ = ("zh", "zl", "x")
GROUP = ("zl", "y", "c")
VMEM = 48 * 1024 * 1024
F32 = jnp.float32
BF16 = jnp.bfloat16


def flip(shard, axis):
    return lax.ppermute(shard, axis, [(0, 1), (1, 0)])


def onward(shard, axis):
    count = lax.axis_size(axis)
    return lax.ppermute(shard, axis, [(i, (i + 1) % count) for i in range(count)])


def rms_rows(values):
    return values * lax.rsqrt(jnp.mean(values * values, axis=-1, keepdims=True) + 1e-06)


def dot(left, right):
    return jnp.dot(left, right, preferred_element_type=F32)


def dot_t(left, right):
    return lax.dot_general(left, right, (((1,), (1,)), ((), ())), preferred_element_type=F32)


def project_kernel(rows_ref, w_ref, out_ref, acc):
    step = pl.program_id(0)
    both, _, toks, wide = rows_ref.shape
    part = dot(rows_ref[...].reshape(both * toks, wide), w_ref[...])

    @pl.when(step == 0)
    def _():
        acc[...] = part

    @pl.when(step > 0)
    def _():
        acc[...] += part

    @pl.when(step == pl.num_programs(0) - 1)
    def _():
        out_ref[...] = acc[...].astype(out_ref.dtype)


def project(rows, w):
    both, parts, toks, wide = rows.shape
    cols = w.shape[1]
    return pl.pallas_call(
        project_kernel,
        grid=(parts,),
        in_specs=[
            pl.BlockSpec((both, 1, toks, wide), lambda m: (0, m, 0, 0)),
            pl.BlockSpec((wide, cols), lambda m: (m, 0)),
        ],
        out_specs=pl.BlockSpec((both * toks, cols), lambda m: (0, 0)),
        out_shape=jax.ShapeDtypeStruct((both * toks, cols), BF16),
        scratch_shapes=[pltpu.VMEM((both * toks, cols), F32)],
        compiler_params=pltpu.CompilerParams(vmem_limit_bytes=VMEM),
        cost_estimate=pl.CostEstimate(
            flops=2 * both * toks * parts * wide * cols,
            bytes_accessed=2 * (rows.size + w.size),
            transcendentals=0,
        ),
    )(rows, w)


def attend_kernel(span, head_dim, lens_ref, q_ref, k_ref, v_ref, attn_ref, prob_ref):
    shard = pl.program_id(0)
    groups = q_ref.shape[1] // span
    heads = q_ref.shape[2] // head_dim
    keys_per = k_ref.shape[1] // groups
    nlen = keys_per // 2
    scale = head_dim ** (-0.5)
    key = lax.broadcasted_iota(jnp.int32, (span, keys_per), 1)
    for g in range(groups):
        base = (shard * groups + g) * 3
        first, second, live = lens_ref[base], lens_ref[base + 1], lens_ref[base + 2]
        mask = jnp.logical_or(key < first, jnp.logical_and(key >= nlen, key < nlen + second))
        weight = live.astype(F32)
        rows, krows = pl.ds(g * span, span), pl.ds(g * keys_per, keys_per)
        for h in range(heads):
            cols = pl.ds(h * head_dim, head_dim)
            scores = dot_t(q_ref[0, rows, cols], k_ref[0, krows, cols]) * scale
            expo = jnp.where(mask, jnp.exp(scores), 0.0)
            prob = expo * (weight / jnp.sum(expo, axis=-1, keepdims=True))
            prob_ref[0, h, rows, :] = prob
            attn = dot(prob.astype(BF16), v_ref[0, krows, cols])
            attn_ref[0, rows, cols] = attn.astype(BF16)


def attend(lens, query, keys, values, span, head_dim):
    shards, toks, inner = query.shape
    krows = keys.shape[1]
    keys_per = krows * span // toks
    heads = inner // head_dim
    qspec = pl.BlockSpec((1, toks, inner), lambda s, lens: (s, 0, 0))
    kspec = pl.BlockSpec((1, krows, inner), lambda s, lens: (s, 0, 0))
    pspec = pl.BlockSpec((1, heads, toks, keys_per), lambda s, lens: (s, 0, 0, 0))
    return pl.pallas_call(
        functools.partial(attend_kernel, span, head_dim),
        grid_spec=pltpu.PrefetchScalarGridSpec(
            num_scalar_prefetch=1,
            grid=(shards,),
            in_specs=[qspec, kspec, kspec],
            out_specs=[qspec, pspec],
        ),
        out_shape=[
            jax.ShapeDtypeStruct((shards, toks, inner), BF16),
            jax.ShapeDtypeStruct((shards, heads, toks, keys_per), F32),
        ],
        compiler_params=pltpu.CompilerParams(vmem_limit_bytes=VMEM),
        cost_estimate=pl.CostEstimate(
            flops=4 * shards * heads * toks * keys_per * head_dim,
            bytes_accessed=2 * (2 * query.size + 2 * keys.size) + 4 * shards * heads * toks * keys_per,
            transcendentals=shards * heads * toks * keys_per,
        ),
    )(lens, query, keys, values)


def backward_kernel(span, head_dim, prob_ref, d_ref, k_ref, v_ref, dq_ref):
    groups = d_ref.shape[1] // span
    heads = d_ref.shape[2] // head_dim
    keys_per = k_ref.shape[1] // groups
    scale = head_dim ** (-0.5)
    for g in range(groups):
        rows, krows = pl.ds(g * span, span), pl.ds(g * keys_per, keys_per)
        for h in range(heads):
            cols = pl.ds(h * head_dim, head_dim)
            prob = prob_ref[0, h, rows, :]
            d_prob = dot_t(d_ref[0, rows, cols], v_ref[0, krows, cols])
            delta = jnp.sum(prob * d_prob, axis=-1, keepdims=True)
            d_score = (prob * (d_prob - delta) * scale).astype(BF16)
            dq_ref[0, rows, cols] = dot(d_score, k_ref[0, krows, cols]).astype(BF16)


def backward(prob, d_attn, keys, values, span, head_dim):
    shards, toks, inner = d_attn.shape
    krows = keys.shape[1]
    heads, keys_per = prob.shape[1], prob.shape[3]
    qspec = pl.BlockSpec((1, toks, inner), lambda s: (s, 0, 0))
    kspec = pl.BlockSpec((1, krows, inner), lambda s: (s, 0, 0))
    pspec = pl.BlockSpec((1, heads, toks, keys_per), lambda s: (s, 0, 0, 0))
    return pl.pallas_call(
        functools.partial(backward_kernel, span, head_dim),
        grid=(shards,),
        in_specs=[pspec, qspec, kspec, kspec],
        out_specs=qspec,
        out_shape=jax.ShapeDtypeStruct((shards, toks, inner), BF16),
        compiler_params=pltpu.CompilerParams(vmem_limit_bytes=VMEM),
        cost_estimate=pl.CostEstimate(
            flops=4 * shards * heads * toks * keys_per * head_dim,
            bytes_accessed=2 * (2 * d_attn.size + 2 * keys.size) + 4 * prob.size,
            transcendentals=0,
        ),
    )(prob, d_attn, keys, values)


def pad_rows(flat, shards, span):
    toks = flat.shape[0] // shards
    return jnp.pad(flat.reshape(shards, toks, flat.shape[1]), ((0, 0), (1, span - 1), (0, 0)))


def unpad_rows(padded, toks):
    return padded[:, 1 : toks + 1].reshape(-1, padded.shape[2])


def sum_heads(rows, w):
    zl, y, c = (lax.axis_index(name) for name in GROUP)
    ny = lax.axis_size("y")
    cols = w.shape[0] // (2 * ny)
    inner = w.shape[1]
    w_parts = w.reshape(ny, 2, cols, inner)

    def part(core):
        return dot_t(rows, lax.dynamic_index_in_dim(w_parts, core, 1, False).reshape(ny * cols, inner))

    sent = flip(part(1 - c).astype(BF16), "c")
    total = part(c) + sent.astype(F32)
    toks = rows.shape[0] // 2
    total = total.reshape(2, toks, ny, cols)
    if ny != 2:
        blocks = total.astype(BF16).transpose(0, 2, 1, 3).reshape(2 * ny * toks, cols)
        return lax.psum_scatter(blocks, ("zl", "y"), scatter_dimension=0, tiled=True).astype(BF16)

    def block(at_zl, at_y):
        return lax.dynamic_slice(total, (at_zl, 0, at_y, 0), (1, toks, 1, cols)).reshape(toks, cols)

    over_both = lax.ppermute(block(1 - zl, 1 - y).astype(BF16), ("zl", "y"), [(i, 3 - i) for i in range(4)])
    over_zl = flip(block(1 - zl, y).astype(BF16), "zl")
    over_y = flip(block(zl, 1 - y).astype(BF16), "y")
    return (
        block(zl, y) + over_zl.astype(F32) + over_y.astype(F32) + over_both.astype(F32)
    ).astype(BF16)


def per_device(
    hidden,
    cotangent,
    neighbour_ids,
    neighbour_lengths,
    embed_table,
    enc_up,
    enc_down,
    w_query,
    w_keyval,
    w_out,
):
    zh, zl, x = (lax.axis_index(name) for name in SEQ)
    y, c = lax.axis_index("y"), lax.axis_index("c")
    nzh, ny = lax.axis_size("zh"), lax.axis_size("y")
    shard = (zh * 2 + zl) * 2 + x
    spans_here, neigh, nlen = neighbour_ids.shape
    toks = hidden.shape[0]
    span = toks // spans_here
    keys_per = neigh * nlen
    groups = spans_here + 1
    rows_here, heads_here, head_dim = w_query.shape
    heads = heads_here // 2
    inner = heads * head_dim
    kv_rows = w_keyval.shape[0]
    seqs = 4 * nzh

    def half(w, which):
        return lax.dynamic_slice_in_dim(w, which * heads, heads, 1)

    def pack_qkv(which):
        kv = half(w_keyval, which)
        return jnp.concatenate(
            [
                half(w_query, which).reshape(rows_here, inner),
                kv[:, :, 0].reshape(kv_rows, inner),
                kv[:, :, 1].reshape(kv_rows, inner),
            ],
            axis=0,
        )

    def pack_out(which):
        return half(w_out, which).reshape(rows_here, inner)

    def gather_weights(pack):
        own, beside = pack(zl), flip(pack(1 - zl), "zl")
        blocks = []
        for hop in range(nzh):
            if hop:
                own, beside = onward(own, "zh"), onward(beside, "zh")
            at = lax.rem(zh + (nzh - hop), nzh)
            for dzl, block in ((0, own), (1, beside)):
                at_zl = lax.rem(zl + dzl, 2)
                blocks.append(((at * 2 + at_zl) * 2 + x, block))
                blocks.append(((at * 2 + at_zl) * 2 + (1 - x), flip(block, "x")))
        return blocks

    def lay_out(blocks, start, size):
        whole = jnp.zeros((seqs * size, inner), BF16)
        for at, block in blocks:
            whole = lax.dynamic_update_slice(whole, block[start : start + size], (at * size, 0))
        return whole

    qkv_blocks = gather_weights(pack_qkv)
    out_blocks = gather_weights(pack_out)
    wq = lay_out(qkv_blocks, 0, rows_here)
    wk = lay_out(qkv_blocks, rows_here, kv_rows)
    wv = lay_out(qkv_blocks, rows_here + kv_rows, kv_rows)
    wo = lay_out(out_blocks, 0, rows_here)

    def gather_tokens(shard_rows):
        whole = lax.all_gather(shard_rows, GROUP, axis=0, tiled=False)
        return whole.reshape(2, 2 * ny, toks, shard_rows.shape[1])

    whole_hidden = gather_tokens(hidden)
    whole_cot = gather_tokens(cotangent)

    ids = neighbour_ids.reshape(spans_here, keys_per)
    ids_before = lax.ppermute(ids[spans_here - 1 :], SEQ, [(i, i + 1) for i in range(seqs - 1)])
    ids = jnp.concatenate([ids_before, ids], axis=0).reshape(groups * keys_per)
    vocab_here = embed_table.shape[0]
    local_ids = ids - (y * 2 + c) * vocab_here
    half_rows = local_ids.shape[0] // 2

    def look_up(core):
        mine = lax.dynamic_slice_in_dim(local_ids, core * half_rows, half_rows, 0)
        inside = jnp.logical_and(mine >= 0, mine < vocab_here)
        picked = jnp.take(embed_table, jnp.clip(mine, 0, vocab_here - 1), axis=0)
        return jnp.where(inside[:, None], picked, jnp.zeros((), picked.dtype))

    emb = look_up(1 - c)
    emb = look_up(c) + flip(emb, "c")
    emb = emb + flip(emb, "y") if ny == 2 else lax.psum(emb, "y")
    emb_wide = emb.astype(F32)
    normed = rms_rows(emb_wide).astype(BF16)
    ffn = jnp.zeros(emb.shape, F32)
    for up, down in ((enc_up, enc_down), (flip(enc_up, "c"), flip(enc_down, "c"))):
        ffn = ffn + dot(jax.nn.gelu(dot_t(normed, up)).astype(BF16), down)
    share_rows = half_rows // ny
    if ny == 2:
        sent = flip(lax.dynamic_slice_in_dim(ffn, (1 - y) * share_rows, share_rows, 0).astype(BF16), "y")
        share = lax.dynamic_slice_in_dim(ffn, y * share_rows, share_rows, 0) + sent.astype(F32)
    else:
        share = lax.psum_scatter(ffn.astype(BF16), "y", scatter_dimension=0, tiled=True).astype(F32)
    emb_share = lax.dynamic_slice_in_dim(emb_wide, y * share_rows, share_rows, 0)
    encoded = rms_rows(emb_share + share).astype(BF16)
    encoded = lax.all_gather(encoded, ("zl", "c", "y"), axis=0, tiled=True)
    keys = dot(encoded, wk).astype(BF16).reshape(2, groups * keys_per, inner)
    values = dot(encoded, wv).astype(BF16).reshape(2, groups * keys_per, inner)

    lens_pad = jnp.concatenate([jnp.ones((1, neigh), jnp.int32), neighbour_lengths], axis=0)
    lens = []
    for at_zl in range(2):
        first = ((zh * 2 + at_zl) * 2 + x) * spans_here
        rows = lax.dynamic_slice_in_dim(lens_pad, first, groups, 0)
        live = (first + jnp.arange(groups, dtype=jnp.int32) > 0).astype(jnp.int32)
        lens.append(jnp.concatenate([rows, live[:, None]], axis=1))
    lens = jnp.stack(lens).reshape(-1)

    query = pad_rows(project(whole_hidden, wq), 2, span)
    attn, prob = attend(lens, query, keys, values, span, head_dim)
    attn = unpad_rows(attn, toks)
    d_attn = pad_rows(project(whole_cot, wo), 2, span)
    d_query = unpad_rows(backward(prob, d_attn, keys, values, span, head_dim), toks)
    hidden_grad = sum_heads(d_query, wq)
    cca_out = sum_heads(attn, wo)
    return (cca_out, hidden_grad)


def solution(mesh):
    ns, nm = mesh.shape["seq"], mesh.shape["mp"]
    fine = Mesh(mesh.devices.reshape(ns // 4, 2, 2, nm // 2, 2), ("zh", "zl", "x", "y", "c"))
    seq, mp = SEQ, ("y", "c")
    return jax.shard_map(
        per_device,
        mesh=fine,
        in_specs=(
            P(seq, mp),
            P(seq, mp),
            P(seq, None, None),
            P(),
            P(mp, None),
            P(mp, None),
            P(mp, None),
            P(seq, mp, None),
            P(seq, mp, None, None),
            P(seq, mp, None),
        ),
        out_specs=(P(seq, mp), P(seq, mp)),
        check_vma=False,
    )
```

```python
import functools

import jax
import jax.numpy as jnp
from jax import lax
from jax.experimental import pallas as pl
from jax.experimental.pallas import tpu as pltpu
from jax.sharding import Mesh
from jax.sharding import PartitionSpec as P

SEQ = ("zh", "zl", "x")
GROUP = ("zl", "y", "c")
VMEM = 62 * 1024 * 1024
F32 = jnp.float32
BF16 = jnp.bfloat16


def flip(shard, axis):
    return lax.ppermute(shard, axis, [(0, 1), (1, 0)])


def onward(shard, axis):
    count = lax.axis_size(axis)
    return lax.ppermute(shard, axis, [(i, (i + 1) % count) for i in range(count)])


def tie(value, *earlier):
    return lax.optimization_barrier((value,) + earlier)[0]


def rms_rows(values):
    return values * lax.rsqrt(jnp.mean(values * values, axis=-1, keepdims=True) + 1e-06)


def dot(left, right):
    return jnp.dot(left, right, preferred_element_type=F32)


def dot_t(left, right):
    return lax.dot_general(left, right, (((1,), (1,)), ((), ())), preferred_element_type=F32)


def call(kernel, grid, prefetch, operands, outs, scratch):
    arrays = [o[0] for o in operands]
    return pl.pallas_call(
        kernel,
        grid_spec=pltpu.PrefetchScalarGridSpec(
            num_scalar_prefetch=1,
            grid=grid,
            in_specs=[pl.BlockSpec(block, index) for _, block, index in operands],
            out_specs=[pl.BlockSpec(block, index) for _, block, index in outs],
            scratch_shapes=scratch,
        ),
        out_shape=[o[0] for o in outs],
        compiler_params=pltpu.CompilerParams(vmem_limit_bytes=VMEM),
        cost_estimate=pl.CostEstimate(flops=1, bytes_accessed=1, transcendentals=0),
    )(prefetch, *arrays)


def shape(dims, dtype):
    return jax.ShapeDtypeStruct(dims, dtype)


def whole_block(ndim):
    return lambda *_: (0,) * ndim


def pack_kernel(
    at_ref, q_ref, kv_ref, o_ref, h_ref, c_ref,
    other_qkv_ref, other_out_ref, own_ref, own_q_ref, own_kv_ref, own_out_ref, states_ref,
    q, kv, o,
):
    rows, inner = own_out_ref.shape
    kv_rows, heads, _, head_dim = kv_ref.shape
    q[...] = q_ref[...].reshape(q.shape)
    o[...] = o_ref[...].reshape(o.shape)
    kv[...] = kv_ref[...].reshape(kv.shape)

    def cut(of, start, size):
        return of[:, pl.ds(pl.multiple_of(start, head_dim), size)]

    def copy(which, q_dst, kv_dst, out_dst):
        q_dst[...] = cut(q, which * inner, inner)
        out_dst[...] = cut(o, which * inner, inner)
        for h in range(heads // 2):
            for i in range(2):
                piece = cut(kv, ((which * (heads // 2) + h) * 2 + i) * head_dim, head_dim)
                kv_dst[i * kv_rows : (i + 1) * kv_rows, h * head_dim : (h + 1) * head_dim] = piece

    zl = at_ref[0]
    kv_end = rows + 2 * kv_rows
    copy(1 - zl, other_qkv_ref.at[:rows], other_qkv_ref.at[rows:], other_out_ref)
    copy(zl, own_ref.at[:rows], own_ref.at[rows:kv_end], own_ref.at[kv_end:])
    copy(zl, own_q_ref, own_kv_ref, own_out_ref)
    states_ref[0] = h_ref[...]
    states_ref[1] = c_ref[...]


def pack(zl, w_query, w_keyval, w_out, hidden, cotangent):
    rows, heads, head_dim = w_query.shape
    kv_rows, inner = w_keyval.shape[0], heads // 2 * head_dim
    sizes = [rows + 2 * kv_rows, rows, 2 * rows + 2 * kv_rows, rows, 2 * kv_rows, rows]
    outs = [(n, inner) for n in sizes] + [(2,) + hidden.shape]
    return call(
        pack_kernel,
        (1,),
        zl.reshape(1),
        [(a, a.shape, whole_block(a.ndim)) for a in (w_query, w_keyval, w_out, hidden, cotangent)],
        [(shape(dims, BF16), dims, whole_block(len(dims))) for dims in outs],
        [pltpu.VMEM(dims, BF16) for dims in ((rows, 2 * inner), (kv_rows, 4 * inner), (rows, 2 * inner))],
    )


def place_kernel(jobs, count, through, at_ref, *refs):
    sources, out_ref, sems = refs[:count], refs[count + through], refs[-1]
    stage = refs[-2] if through else out_ref

    def dst(ref, i, rows, plane):
        to = pl.ds(pl.multiple_of(at_ref[i] * rows, 16), rows)
        return ref.at[to] if plane is None else ref.at[plane, to]

    copies = []
    for i, (source, start, rows, plane) in enumerate(jobs):
        src = sources[source].at[pl.ds(start, rows)]
        to = stage.at[pl.ds(i * rows, rows)] if through else dst(stage, i, rows, plane)
        copies.append(pltpu.make_async_copy(src, to, sems.at[i]))
    for copy in copies:
        copy.start()
    for copy in copies:
        copy.wait()
    if through:
        copies = []
        for i, (_, _, rows, plane) in enumerate(jobs):
            src = stage.at[pl.ds(i * rows, rows)]
            copies.append(pltpu.make_async_copy(src, dst(out_ref, i, rows, plane), sems.at[i]))
        for copy in copies:
            copy.start()
        for copy in copies:
            copy.wait()


def place(pieces, dims, base=None):
    sources = []
    for piece in pieces:
        if not any(piece[1] is a for a in sources):
            sources.append(piece[1])
    index = [next(i for i, a in enumerate(sources) if a is piece[1]) for piece in pieces]
    jobs = [(i, p[2], p[3], p[4]) for i, p in zip(index, pieces)]
    if any(rows % 16 for _, _, rows, _ in jobs):
        whole = jnp.zeros(dims, BF16) if base is None else base
        for (at, block, start, rows, plane) in pieces:
            block = block[start : start + rows]
            if plane is None:
                whole = lax.dynamic_update_slice(whole, block, (at * rows, 0))
            else:
                whole = lax.dynamic_update_slice(whole, block[None], (plane, at * rows, 0))
        return whole
    through = base is not None
    arrays = sources + [base] if through else sources
    scratch = [pltpu.SemaphoreType.DMA((len(jobs),))]
    if through:
        scratch.insert(0, pltpu.VMEM((len(jobs) * jobs[0][2], dims[-1]), BF16))
    out_spec = pl.BlockSpec(memory_space=pl.ANY) if through else pl.BlockSpec(dims, whole_block(len(dims)))
    return pl.pallas_call(
        functools.partial(place_kernel, jobs, len(sources), int(through)),
        grid_spec=pltpu.PrefetchScalarGridSpec(
            num_scalar_prefetch=1,
            grid=(1,),
            in_specs=[pl.BlockSpec(memory_space=pl.ANY)] * len(arrays),
            out_specs=out_spec,
            scratch_shapes=scratch,
        ),
        out_shape=shape(dims, BF16),
        input_output_aliases={len(arrays): 0} if through else {},
        compiler_params=pltpu.CompilerParams(vmem_limit_bytes=VMEM),
        cost_estimate=pl.CostEstimate(flops=1, bytes_accessed=1, transcendentals=0),
    )(jnp.stack([p[0] for p in pieces]).astype(jnp.int32), *arrays)


def project_kernel(span, first, last, at_ref, own_ref, other_ref, w_ref, *rest):
    out_ref, acc = rest[-2:]
    step = pl.program_id(0)
    toks, cols = own_ref.shape[0], acc.shape[1]
    rows = jnp.concatenate([own_ref[...], other_ref[...]], axis=0)
    part = dot(rows, w_ref[...])

    @pl.when(step == 0)
    def _():
        acc[...] = part if first else part + rest[0][...]

    @pl.when(step > 0)
    def _():
        acc[...] += part

    @pl.when(step == pl.num_programs(0) - 1)
    def _():
        if not last:
            out_ref[...] = acc[...]
            return
        front, back = jnp.zeros((1, cols), F32), jnp.zeros((span - 1, cols), F32)
        for s in range(2):
            own = acc[s * toks : (s + 1) * toks, :]
            out_ref[s] = jnp.concatenate([front, own, back], axis=0).astype(BF16)


def project(at, states, which, w, wide, span, last, before=None):
    toks, wm = states[1].shape[1:]
    cols, steps, per = w.shape[1], at.shape[0], wm // wide
    operands = [
        (states[0], (None, None, toks, wide), lambda i, at: (at[i] // per, which, 0, lax.rem(at[i], per))),
        (states[1], (None, toks, wide), lambda i, at: (at[i] // per, 0, lax.rem(at[i], per))),
        (w, (wide, cols), lambda i, at: (at[i], 0)),
    ]
    total = (2 * toks, cols)
    if before is not None:
        operands.append((before, total, whole_block(2)))
    out = shape((2, toks + span, cols), BF16) if last else shape(total, F32)
    return call(
        functools.partial(project_kernel, span, before is None, last),
        (steps,),
        at,
        operands,
        [(out, out.shape, whole_block(len(out.shape)))],
        [pltpu.VMEM(total, F32)],
    )[0]


def keyval_kernel(at_ref, own_ref, other_ref, w_ref, k_ref, v_ref):
    for turn, rows_ref in enumerate((own_ref, other_ref)):

        @pl.when(pl.program_id(0) == turn)
        def _():
            rows = rows_ref[...]
            k_ref[...] = dot(rows, w_ref[0]).astype(BF16)
            v_ref[...] = dot(rows, w_ref[1]).astype(BF16)


def keyval(at, own, other, w):
    count, width = own.shape
    inner = w.shape[2]
    out = (shape((2 * count, inner), BF16), (count, inner), lambda i, at: (i, 0))
    operands = [(a, a.shape, whole_block(a.ndim)) for a in (own, other, w)]
    return call(keyval_kernel, (2,), at, operands, [out, out], [])


def encode_kernel(at_ref, emb_ref, up_ref, down_ref, up2_ref, down2_ref, ffn_ref, own_ref, normed, acc):
    step = pl.program_id(0)

    @pl.when(step == 0)
    def _():
        normed[...] = rms_rows(emb_ref[...].astype(F32)).astype(BF16)

    part = 0.0
    for up, down in ((up_ref, down_ref), (up2_ref, down2_ref)):
        act = jax.nn.gelu(dot_t(normed[...], up[...])).astype(BF16)
        part = part + dot(act, down[...])

    @pl.when(step == 0)
    def _():
        acc[...] = part

    @pl.when(step > 0)
    def _():
        acc[...] += part

    @pl.when(step == pl.num_programs(0) - 1)
    def _():
        share = own_ref.shape[0]
        ffn_ref[...] = acc[...].astype(BF16)
        mine = pl.ds(pl.multiple_of(at_ref[0] * share, share), share)
        own_ref[...] = acc[mine, :] + emb_ref[mine, :].astype(F32)


def encode(y, emb, weights, share, tiles):
    count, width = emb.shape
    hidden = weights[0].shape[0]
    tile = hidden // tiles
    return call(
        encode_kernel,
        (tiles,),
        y.reshape(1),
        [(emb, emb.shape, whole_block(2))]
        + [(w, (tile, width), lambda i, at: (i, 0)) for w in weights],
        [
            (shape((count, width), BF16), (count, width), whole_block(2)),
            (shape((share, width), F32), (share, width), whole_block(2)),
        ],
        [pltpu.VMEM((count, width), BF16), pltpu.VMEM((count, width), F32)],
    )


def span_rows(halves, g, cols):
    parts = [half[0, :, g, :, cols] for half in halves]
    parts = [p.reshape(p.shape[0] * p.shape[1], p.shape[2]) for p in parts]
    return jnp.concatenate(parts, axis=0)


def attend_kernel(span, head_dim, at_ref, q_ref, k_ref, v_ref, k2_ref, v2_ref, attn_ref, prob_ref, stage):
    turn = pl.program_id(0)
    _, blocks, groups, piece, inner = k_ref.shape
    heads, keys_per = inner // head_dim, 2 * blocks * piece
    nlen = keys_per // 2
    scale = head_dim ** (-0.5)
    toks = attn_ref.shape[1]
    lane = lax.broadcasted_iota(jnp.int32, (span, keys_per), 1)
    key = lane
    for i in range(2 * blocks):
        start = at_ref[2 * groups * 3 + i]
        here = jnp.logical_and(lane >= i * piece, lane < (i + 1) * piece)
        key = jnp.where(here, lane + (start - i * piece), key)
    for g in range(groups):
        rows = pl.ds(g * span, span)
        for h in range(heads):
            cols = pl.ds(h * head_dim, head_dim)
            prob_ref[0, h, rows, :] = dot_t(q_ref[0, rows, cols], span_rows((k_ref, k2_ref), g, cols))
    for g in range(groups):
        rows = pl.ds(g * span, span)
        base = (turn * groups + g) * 3
        first, second, live = at_ref[base], at_ref[base + 1], at_ref[base + 2]
        mask = jnp.logical_or(key < first, jnp.logical_and(key >= nlen, key < nlen + second))
        weight = live.astype(F32)
        for h in range(heads):
            cols = pl.ds(h * head_dim, head_dim)
            expo = jnp.where(mask, jnp.exp(prob_ref[0, h, rows, :] * scale), 0.0)
            prob = expo * (weight / jnp.sum(expo, axis=-1, keepdims=True))
            prob_ref[0, h, rows, :] = prob
            stage[rows, cols] = dot(prob.astype(BF16), span_rows((v_ref, v2_ref), g, cols))
    attn_ref[0] = stage[1 : toks + 1, :].astype(BF16)


def backward_kernel(
    span, head_dim, at_ref, prob_ref, d_ref, k_ref, v_ref, k2_ref, v2_ref, dq_ref, stage, d_prob
):
    groups, inner = k_ref.shape[2], k_ref.shape[4]
    heads = inner // head_dim
    scale = head_dim ** (-0.5)
    toks = dq_ref.shape[1]
    for g in range(groups):
        rows = pl.ds(g * span, span)
        for h in range(heads):
            cols = pl.ds(h * head_dim, head_dim)
            d_prob[h, rows, :] = dot_t(d_ref[0, rows, cols], span_rows((v_ref, v2_ref), g, cols))
    for g in range(groups):
        rows = pl.ds(g * span, span)
        for h in range(heads):
            cols = pl.ds(h * head_dim, head_dim)
            prob, slope = prob_ref[0, h, rows, :], d_prob[h, rows, :]
            delta = jnp.sum(prob * slope, axis=-1, keepdims=True)
            d_score = (prob * (slope - delta) * scale).astype(BF16)
            stage[rows, cols] = dot(d_score, span_rows((k_ref, k2_ref), g, cols))
    dq_ref[0] = stage[1 : toks + 1, :].astype(BF16)


def over_shards(kernel, at, padded, kv, span, head_dim, prob):
    shards, rows, inner = padded.shape
    toks = rows - span
    keys_per = 2 * kv[0].shape[1] * kv[0].shape[3]
    heads = inner // head_dim
    def by_turn(ndim):
        return lambda s, at: (s,) + (0,) * (ndim - 1)

    probs = shape((shards, heads, rows, keys_per), F32)
    prob_spec = ((1, heads, rows, keys_per), by_turn(4))
    operands = [(padded, (1, rows, inner), by_turn(3))]
    operands += [(a, (1,) + a.shape[1:], by_turn(5)) for a in kv]
    outs = [(shape((shards, toks, inner), BF16), (1, toks, inner), by_turn(3))]
    scratch = [pltpu.VMEM((rows, inner), F32)]
    if prob is None:
        outs.append((probs,) + prob_spec)
    else:
        operands.insert(0, (prob,) + prob_spec)
        scratch.append(pltpu.VMEM(probs.shape[1:], F32))
    return call(functools.partial(kernel, span, head_dim), (shards,), at, operands, outs, scratch)


def sent_kernel(at_ref, rows_ref, w_ref, out_ref):
    out_ref[0] = dot_t(rows_ref[...], w_ref[...]).astype(BF16)


def kept_kernel(at_ref, rows_ref, w_ref, add_ref, both_ref, y_ref, zl_ref, own_ref):
    total = dot_t(rows_ref[...], w_ref[...]) + add_ref[0].astype(F32)
    toks = own_ref.shape[0]

    @pl.when(pl.program_id(0) == 0)
    def _():
        y_ref[...] = total[:toks].astype(BF16)
        both_ref[...] = total[toks:].astype(BF16)

    @pl.when(pl.program_id(0) == 1)
    def _():
        own_ref[...] = total[:toks]
        zl_ref[...] = total[toks:].astype(BF16)


CUTS = 1


def columns(at, rows, w, wm, add=None):
    count, inner = rows.shape
    cut = wm // CUTS
    operands = [
        (rows, rows.shape, whole_block(2)),
        (w, (cut, inner), lambda i, j, at: (at[i] * CUTS + j, 0)),
    ]
    moved = (1, count, cut), lambda i, j, at: (i, 0, j)
    if add is None:
        out = shape((2, count, wm), BF16)
        return call(sent_kernel, (2, CUTS), at, operands, [(out,) + moved], [])[0]
    operands.append((add,) + moved)
    half = (count // 2, wm)
    block = (count // 2, cut)
    early = lambda i, j, at: (0, jnp.where(i == 0, j, CUTS - 1))
    late = lambda i, j, at: (0, jnp.where(i == 0, 0, j))
    outs = [(shape(half, BF16), block, early)] * 2
    outs += [(shape(half, BF16), block, late), (shape(half, F32), block, late)]
    return call(kept_kernel, (2, CUTS), at, operands, outs, [])


def core_sums(rows, w):
    y, c = lax.axis_index("y"), lax.axis_index("c")
    ny = lax.axis_size("y")
    wm = w.shape[0] // (2 * ny)
    if ny != 2:
        return None
    return columns(jnp.stack([(1 - y) * 2 + (1 - c), y * 2 + (1 - c)]), rows, w, wm)


def sum_heads(rows, w, sent):
    zl, y, c = (lax.axis_index(name) for name in GROUP)
    ny = lax.axis_size("y")
    wm = w.shape[0] // (2 * ny)
    count = rows.shape[0]
    if ny != 2:
        rows = jnp.roll(rows, zl * (count // 2), axis=0)
        blocks = dot_t(rows, w).astype(BF16).reshape(2, count // 2, ny, 2, wm)
        blocks = blocks.transpose(0, 2, 3, 1, 4).reshape(ny * 2 * count, wm)
        return lax.psum_scatter(blocks, GROUP, scatter_dimension=0, tiled=True).astype(BF16), ()
    at = jnp.stack([(1 - y) * 2 + c, y * 2 + c])
    to_both, to_y, to_zl, own = columns(at, rows, w, wm, flip(sent, "c"))
    over_both = lax.ppermute(to_both, ("zl", "y"), [(i, 3 - i) for i in range(4)])
    over_y, over_zl = flip(to_y, "y"), flip(to_zl, "zl")
    total = own + over_zl.astype(F32) + over_y.astype(F32) + over_both.astype(F32)
    return total.astype(BF16), (to_both, to_y, to_zl)


def per_device(
    hidden,
    cotangent,
    neighbour_ids,
    neighbour_lengths,
    embed_table,
    enc_up,
    enc_down,
    w_query,
    w_keyval,
    w_out,
):
    zh, zl, x = (lax.axis_index(name) for name in SEQ)
    y, c = lax.axis_index("y"), lax.axis_index("c")
    nzh, ny = lax.axis_size("zh"), lax.axis_size("y")
    spans_here, neigh, nlen = neighbour_ids.shape
    toks = hidden.shape[0]
    span = toks // spans_here
    keys_per = neigh * nlen
    groups = spans_here + 1
    rows_here, heads_here, head_dim = w_query.shape
    heads = heads_here // 2
    inner = heads * head_dim
    kv_rows, enc_width = w_keyval.shape[0], embed_table.shape[1]
    seqs = 4 * nzh
    piece = keys_per // (2 * ny)

    qkv_rows = rows_here + 2 * kv_rows

    def shard_at(hop, at_zl, at_x):
        return (lax.rem(zh + (nzh - hop), nzh) * 2 + at_zl) * 2 + at_x

    packed = pack(zl, w_query, w_keyval, w_out, hidden, cotangent)
    other_qkv, other_out, own, own_q, own_kv, own_out, states = packed
    up2, down2 = flip(enc_up, "c"), flip(enc_down, "c")
    beside_qkv = flip(other_qkv, "zl")
    own_x = flip(own, "x")
    hop_q = onward(own_q, "zh")

    def gather_states(rows):
        return lax.all_gather(rows, ("y", "c"), axis=0, tiled=False)

    own_states = gather_states(states)

    ids = neighbour_ids.reshape(spans_here, 2, ny, piece).transpose(1, 2, 0, 3).reshape(-1)
    vocab_here = embed_table.shape[0]
    local_ids = tie(ids, other_qkv) - (y * 2 + c) * vocab_here
    inside = jnp.logical_and(local_ids >= 0, local_ids < vocab_here)
    clipped = jnp.clip(local_ids, 0, vocab_here - 1)
    picked = tie(embed_table.at[clipped].get(mode="promise_in_bounds"), hop_q, beside_qkv, up2, down2)
    half_rows = ids.shape[0] // 2

    def half_emb(core):
        rows = lax.dynamic_slice_in_dim(picked, core * half_rows, half_rows, 0)
        live = lax.dynamic_slice_in_dim(inside, core * half_rows, half_rows, 0)
        return jnp.where(live[:, None], rows, jnp.zeros((), BF16))

    emb_other = half_emb(1 - c)
    emb = tie(half_emb(c), own_x) + flip(emb_other, "c")

    beside_qkv, other_out, hop_q = (tie(a, emb) for a in (beside_qkv, other_out, hop_q))
    beside_qkv_x, hop_q_x = flip(beside_qkv, "x"), flip(hop_q, "x")
    hop_q2 = onward(beside_qkv[:rows_here], "zh")
    beside_out = flip(other_out, "zl")
    emb = emb + flip(emb, "y") if ny == 2 else lax.psum(emb, "y")
    emb = tie(emb, beside_qkv_x, hop_q_x, hop_q2, beside_out, own_states)

    own_kv, beside_out, hidden = (tie(a, emb) for a in (own_kv, beside_out, hidden))
    hop_kv = onward(own_kv, "zh")
    beside_out_x = flip(beside_out, "x")
    other_hidden = flip(hidden, "zl")
    share_rows = half_rows // ny
    ffn, share = encode(y, emb, [enc_up, enc_down, up2, down2], share_rows, 2)
    ffn = tie(ffn, hop_kv)
    hop_kv2 = onward(tie(beside_qkv, ffn)[rows_here:], "zh")
    if ny == 2:
        sent = lax.dynamic_slice_in_dim(ffn, (1 - y) * share_rows, share_rows, 0)
        share = share + flip(sent, "y").astype(F32)
    else:
        share = lax.psum_scatter(ffn, "y", scatter_dimension=0, tiled=True).astype(F32)
        share = share + lax.dynamic_slice_in_dim(emb, y * share_rows, share_rows, 0).astype(F32)
    encoded = rms_rows(tie(share, beside_out_x, other_hidden)).astype(BF16)

    other_hidden = gather_states(tie(other_hidden, encoded))
    before = lax.ppermute(encoded[share_rows - piece :], SEQ, [(i, i + 1) for i in range(seqs - 1)])
    encoded = jnp.concatenate([tie(before, hop_kv2), encoded], axis=0)
    hop_qkv = jnp.concatenate([tie(hop_q2, encoded), hop_kv, hop_kv2], axis=0)
    hop_qkv_x = flip(hop_qkv, "x")
    hop_out = onward(jnp.concatenate([tie(own_out, encoded), beside_out], axis=0), "zh")

    if ny == 2:
        corner = lax.ppermute(encoded, ("zl", "y"), [(i, 3 - i) for i in range(4)])
        over_y, over_zl = flip(encoded, "y"), flip(encoded, "zl")
        over_y = tie(over_y, hop_qkv_x)
        own_rows, other_rows = [encoded, over_y], [over_zl, tie(corner, hop_out)]
        ys = [y, 1 - y]
    else:
        own_rows = [lax.all_gather(encoded, "y", axis=0, tiled=True)]
        other_rows, over_y = [flip(own_rows[0], "zl")], own_rows[0]
        ys = [jnp.int32(i) for i in range(ny)]

    q_pieces, kv_pieces, out_pieces = [], [], []

    def add_kv(at, block, start):
        kv_pieces.append((at, block, start, kv_rows, 0))
        kv_pieces.append((at, block, start + kv_rows, kv_rows, 1))

    here, here_x = shard_at(0, zl, x), shard_at(0, zl, 1 - x)
    there, there_x = shard_at(0, 1 - zl, x), shard_at(0, 1 - zl, 1 - x)
    for at, block, start in ((here, own_q, 0), (here_x, own_x, 0), (there, beside_qkv, 0), (there_x, beside_qkv_x, 0)):
        q_pieces.append((at, block, start, rows_here, None))
    for at, block, start in (
        (here, own_kv, 0),
        (here_x, own_x, rows_here),
        (there, beside_qkv, rows_here),
        (there_x, beside_qkv_x, rows_here),
    ):
        add_kv(at, block, start)
    for at, block, start in ((here, own_out, 0), (here_x, own_x, qkv_rows), (there, beside_out, 0), (there_x, beside_out_x, 0)):
        out_pieces.append((at, block, start, rows_here, None))
    for hop in range(1, nzh):
        if hop > 1:
            hop_q, hop_qkv = onward(hop_q, "zh"), onward(hop_qkv, "zh")
            hop_q_x, hop_qkv_x = flip(hop_q, "x"), flip(hop_qkv, "x")
        for at_x, at_q, at_qkv in ((x, hop_q, hop_qkv), (1 - x, hop_q_x, hop_qkv_x)):
            here, there = shard_at(hop, zl, at_x), shard_at(hop, 1 - zl, at_x)
            q_pieces += [(here, at_q, 0, rows_here, None), (there, at_qkv, 0, rows_here, None)]
            add_kv(here, at_qkv, rows_here)
            add_kv(there, at_qkv, qkv_rows)

    lens_pad = jnp.concatenate([jnp.ones((1, neigh), jnp.int32), neighbour_lengths], axis=0)
    at = []
    for turn in range(2):
        first = ((zh * 2 + lax.rem(zl + turn, 2)) * 2 + x) * spans_here
        rows = lax.dynamic_slice_in_dim(lens_pad, first, groups, 0)
        live = (first + jnp.arange(groups, dtype=jnp.int32) > 0).astype(jnp.int32)
        at.append(jnp.concatenate([rows, live[:, None]], axis=1).reshape(-1))
    starts = [(core * ny + at_y) * piece for core in (c, 1 - c) for at_y in ys]
    at = jnp.concatenate(at + [jnp.stack(starts).astype(jnp.int32)])

    w_dims = (seqs * rows_here, inner)
    q_pieces[0] = (q_pieces[0][0], tie(q_pieces[0][1], over_y)) + q_pieces[0][2:]
    kv_pieces[0] = (kv_pieces[0][0], tie(kv_pieces[0][1], over_y)) + kv_pieces[0][2:]
    wkv = place(kv_pieces, (2, enc_width, inner))
    own_rows = jnp.concatenate(own_rows, axis=0)
    own_rows2 = flip(own_rows, "c")
    other_rows = jnp.concatenate([tie(other_rows[0], wkv)] + other_rows[1:], axis=0)
    other_rows2 = flip(other_rows, "c")
    hop_out = tie(hop_out, other_rows)
    hop_out_x = flip(hop_out, "x")
    other_cot = flip(tie(cotangent, other_rows), "zl")
    wq = place(q_pieces, w_dims)
    every = jnp.arange(2 * ny, dtype=jnp.int32)
    kv_shape = (2, ny, groups, piece, inner)
    keys, values = keyval(at, own_rows, other_rows, wkv)
    other_cot = gather_states(tie(other_cot, keys))
    other_rows2 = tie(other_rows2, keys)
    keys2, values2 = keyval(at, own_rows2, other_rows2, wkv)
    query = project(every, (own_states, other_hidden), 0, tie(wq, keys2), hidden.shape[1], span, True)
    kv = [a.reshape(kv_shape) for a in (keys, values, keys2, values2)]
    attn, prob = over_shards(attend_kernel, at, query, kv, span, head_dim, None)
    attn = attn.reshape(2 * toks, inner)

    late = []
    for hop in range(1, nzh):
        if hop > 1:
            hop_out = onward(hop_out, "zh")
            hop_out_x = flip(hop_out, "x")
        for at_x, block in ((x, hop_out), (1 - x, hop_out_x)):
            late.append((shard_at(hop, zl, at_x), block, 0, rows_here, None))
            late.append((shard_at(hop, 1 - zl, at_x), block, rows_here, rows_here, None))

    def at_of(pieces):
        return jnp.stack([p[0] for p in pieces])

    states = (own_states, other_cot)
    wo = place(out_pieces, w_dims)
    some = project(at_of(out_pieces), states, 1, tie(wo, attn), rows_here, span, False)
    hop_out_x = tie(hop_out_x, some)
    late[-2:] = [(p[0], hop_out_x) + p[2:] for p in late[-2:]]
    wo = place(late, w_dims, wo)
    out_sent = core_sums(attn, wo)
    if out_sent is not None:
        some = tie(some, out_sent)
    d_attn = project(at_of(late), states, 1, wo, rows_here, span, True, some)
    cca_out, moved = sum_heads(tie(attn, d_attn), wo, out_sent)
    (d_query,) = over_shards(backward_kernel, at, tie(d_attn, *moved), kv, span, head_dim, prob)
    d_query = d_query.reshape(2 * toks, inner)
    hidden_grad, _ = sum_heads(d_query, wq, core_sums(d_query, wq))
    return (cca_out, hidden_grad)


def solution(mesh):
    ns, nm = mesh.shape["seq"], mesh.shape["mp"]
    fine = Mesh(mesh.devices.reshape(ns // 4, 2, 2, nm // 2, 2), ("zh", "zl", "x", "y", "c"))
    seq, mp = SEQ, ("y", "c")
    return jax.shard_map(
        per_device,
        mesh=fine,
        in_specs=(
            P(seq, mp),
            P(seq, mp),
            P(seq, None, None),
            P(),
            P(mp, None),
            P(mp, None),
            P(mp, None),
            P(seq, mp, None),
            P(seq, mp, None, None),
            P(seq, mp, None),
        ),
        out_specs=(P(seq, mp), P(seq, mp)),
        check_vma=False,
    )
```

```python
import functools

import jax
import jax.numpy as jnp
from jax import lax
from jax.experimental import pallas as pl
from jax.experimental.pallas import tpu as pltpu
from jax.sharding import Mesh
from jax.sharding import PartitionSpec as P

SEQ = ("zh", "zl", "x")
GROUP = ("zl", "y", "c")
VMEM = 62 * 1024 * 1024
F32 = jnp.float32
BF16 = jnp.bfloat16


def flip(shard, axis):
    return lax.ppermute(shard, axis, [(0, 1), (1, 0)])


def onward(shard, axis):
    count = lax.axis_size(axis)
    return lax.ppermute(shard, axis, [(i, (i + 1) % count) for i in range(count)])


def tie(value, *earlier):
    return lax.optimization_barrier((value,) + earlier)[0]


def rms_rows(values):
    return values * lax.rsqrt(jnp.mean(values * values, axis=-1, keepdims=True) + 1e-06)


def dot(left, right):
    return jnp.dot(left, right, preferred_element_type=F32)


def dot_t(left, right):
    return lax.dot_general(left, right, (((1,), (1,)), ((), ())), preferred_element_type=F32)


def call(kernel, grid, prefetch, operands, outs, scratch):
    arrays = [o[0] for o in operands]
    return pl.pallas_call(
        kernel,
        grid_spec=pltpu.PrefetchScalarGridSpec(
            num_scalar_prefetch=1,
            grid=grid,
            in_specs=[pl.BlockSpec(block, index) for _, block, index in operands],
            out_specs=[pl.BlockSpec(block, index) for _, block, index in outs],
            scratch_shapes=scratch,
        ),
        out_shape=[o[0] for o in outs],
        compiler_params=pltpu.CompilerParams(vmem_limit_bytes=VMEM),
        cost_estimate=pl.CostEstimate(flops=20000000000, bytes_accessed=1, transcendentals=0),
    )(prefetch, *arrays)


def shape(dims, dtype):
    return jax.ShapeDtypeStruct(dims, dtype)


def whole_block(ndim):
    return lambda *_: (0,) * ndim


def pack_kernel(
    at_ref, q_ref, kv_ref, o_ref, h_ref, c_ref,
    other_qkv_ref, other_out_ref, own_ref, own_q_ref, own_kv_ref, own_out_ref, states_ref,
    q, kv, o,
):
    rows, inner = own_out_ref.shape
    kv_rows, heads, _, head_dim = kv_ref.shape
    q[...] = q_ref[...].reshape(q.shape)
    o[...] = o_ref[...].reshape(o.shape)
    kv[...] = kv_ref[...].reshape(kv.shape)

    def cut(of, start, size):
        return of[:, pl.ds(pl.multiple_of(start, head_dim), size)]

    def copy(which, q_dst, kv_dst, out_dst):
        q_dst[...] = cut(q, which * inner, inner)
        out_dst[...] = cut(o, which * inner, inner)
        for h in range(heads // 2):
            for i in range(2):
                piece = cut(kv, ((which * (heads // 2) + h) * 2 + i) * head_dim, head_dim)
                kv_dst[i * kv_rows : (i + 1) * kv_rows, h * head_dim : (h + 1) * head_dim] = piece

    zl = at_ref[0]
    kv_end = rows + 2 * kv_rows
    copy(1 - zl, other_qkv_ref.at[:rows], other_qkv_ref.at[rows:], other_out_ref)
    copy(zl, own_ref.at[:rows], own_ref.at[rows:kv_end], own_ref.at[kv_end:])
    copy(zl, own_q_ref, own_kv_ref, own_out_ref)
    states_ref[0] = h_ref[...]
    states_ref[1] = c_ref[...]


def pack(zl, w_query, w_keyval, w_out, hidden, cotangent):
    rows, heads, head_dim = w_query.shape
    kv_rows, inner = w_keyval.shape[0], heads // 2 * head_dim
    sizes = [rows + 2 * kv_rows, rows, 2 * rows + 2 * kv_rows, rows, 2 * kv_rows, rows]
    outs = [(n, inner) for n in sizes] + [(2,) + hidden.shape]
    return call(
        pack_kernel,
        (1,),
        zl.reshape(1),
        [(a, a.shape, whole_block(a.ndim)) for a in (w_query, w_keyval, w_out, hidden, cotangent)],
        [(shape(dims, BF16), dims, whole_block(len(dims))) for dims in outs],
        [pltpu.VMEM(dims, BF16) for dims in ((rows, 2 * inner), (kv_rows, 4 * inner), (rows, 2 * inner))],
    )


def place_kernel(jobs, count, through, at_ref, *refs):
    sources, out_ref, sems = refs[:count], refs[count + through], refs[-1]
    stage = refs[-2] if through else out_ref

    def dst(ref, i, rows, plane):
        to = pl.ds(pl.multiple_of(at_ref[i] * rows, 16), rows)
        return ref.at[to] if plane is None else ref.at[plane, to]

    copies = []
    for i, (source, start, rows, plane) in enumerate(jobs):
        src = sources[source].at[pl.ds(start, rows)]
        to = stage.at[pl.ds(i * rows, rows)] if through else dst(stage, i, rows, plane)
        copies.append(pltpu.make_async_copy(src, to, sems.at[i]))
    for copy in copies:
        copy.start()
    for copy in copies:
        copy.wait()
    if through:
        copies = []
        for i, (_, _, rows, plane) in enumerate(jobs):
            src = stage.at[pl.ds(i * rows, rows)]
            copies.append(pltpu.make_async_copy(src, dst(out_ref, i, rows, plane), sems.at[i]))
        for copy in copies:
            copy.start()
        for copy in copies:
            copy.wait()


def place(pieces, dims, base=None):
    sources = []
    for piece in pieces:
        if not any(piece[1] is a for a in sources):
            sources.append(piece[1])
    index = [next(i for i, a in enumerate(sources) if a is piece[1]) for piece in pieces]
    jobs = [(i, p[2], p[3], p[4]) for i, p in zip(index, pieces)]
    if any(rows % 16 for _, _, rows, _ in jobs):
        whole = jnp.zeros(dims, BF16) if base is None else base
        for (at, block, start, rows, plane) in pieces:
            block = block[start : start + rows]
            if plane is None:
                whole = lax.dynamic_update_slice(whole, block, (at * rows, 0))
            else:
                whole = lax.dynamic_update_slice(whole, block[None], (plane, at * rows, 0))
        return whole
    through = base is not None
    arrays = sources + [base] if through else sources
    scratch = [pltpu.SemaphoreType.DMA((len(jobs),))]
    if through:
        scratch.insert(0, pltpu.VMEM((len(jobs) * jobs[0][2], dims[-1]), BF16))
    out_spec = pl.BlockSpec(memory_space=pl.ANY) if through else pl.BlockSpec(dims, whole_block(len(dims)))
    return pl.pallas_call(
        functools.partial(place_kernel, jobs, len(sources), int(through)),
        grid_spec=pltpu.PrefetchScalarGridSpec(
            num_scalar_prefetch=1,
            grid=(1,),
            in_specs=[pl.BlockSpec(memory_space=pl.ANY)] * len(arrays),
            out_specs=out_spec,
            scratch_shapes=scratch,
        ),
        out_shape=shape(dims, BF16),
        input_output_aliases={len(arrays): 0} if through else {},
        compiler_params=pltpu.CompilerParams(vmem_limit_bytes=VMEM),
        cost_estimate=pl.CostEstimate(flops=20000000000, bytes_accessed=1, transcendentals=0),
    )(jnp.stack([p[0] for p in pieces]).astype(jnp.int32), *arrays)


def project_kernel(span, first, last, at_ref, own_ref, other_ref, w_ref, *rest):
    out_ref, acc = rest[-2:]
    step = pl.program_id(0)
    toks, cols = own_ref.shape[0], acc.shape[1]
    rows = jnp.concatenate([own_ref[...], other_ref[...]], axis=0)
    part = dot(rows, w_ref[...])

    @pl.when(step == 0)
    def _():
        acc[...] = part if first else part + rest[0][...]

    @pl.when(step > 0)
    def _():
        acc[...] += part

    @pl.when(step == pl.num_programs(0) - 1)
    def _():
        if not last:
            out_ref[...] = acc[...]
            return
        front, back = jnp.zeros((1, cols), F32), jnp.zeros((span - 1, cols), F32)
        for s in range(2):
            own = acc[s * toks : (s + 1) * toks, :]
            out_ref[s] = jnp.concatenate([front, own, back], axis=0).astype(BF16)


def project(at, states, which, w, wide, span, last, before=None):
    toks, wm = states[0].shape[2:]
    cols, steps, per = w.shape[1], at.shape[0], wm // wide
    operands = [
        (a, (None, None, toks, wide), lambda i, at: (at[i] // per, which, 0, lax.rem(at[i], per)))
        for a in states
    ]
    operands += [
        (w, (wide, cols), lambda i, at: (at[i], 0)),
    ]
    total = (2 * toks, cols)
    if before is not None:
        operands.append((before, total, whole_block(2)))
    out = shape((2, toks + span, cols), BF16) if last else shape(total, F32)
    return call(
        functools.partial(project_kernel, span, before is None, last),
        (steps,),
        at,
        operands,
        [(out, out.shape, whole_block(len(out.shape)))],
        [pltpu.VMEM(total, F32)],
    )[0]


def keyval_kernel(at_ref, rows_ref, w_ref, k_ref, v_ref):
    rows = rows_ref[...]
    k_ref[...] = dot(rows, w_ref[0]).astype(BF16)
    v_ref[...] = dot(rows, w_ref[1]).astype(BF16)


def keyval(at, rows, w):
    out = shape((rows.shape[0], w.shape[2]), BF16)
    operands = [(a, a.shape, whole_block(a.ndim)) for a in (rows, w)]
    return call(keyval_kernel, (1,), at, operands, [(out, out.shape, whole_block(2))] * 2, [])


def encode_kernel(at_ref, emb_ref, up_ref, down_ref, up2_ref, down2_ref, ffn_ref, own_ref, normed, acc):
    step = pl.program_id(0)

    @pl.when(step == 0)
    def _():
        normed[...] = rms_rows(emb_ref[...].astype(F32)).astype(BF16)

    part = 0.0
    for up, down in ((up_ref, down_ref), (up2_ref, down2_ref)):
        act = jax.nn.gelu(dot_t(normed[...], up[...])).astype(BF16)
        part = part + dot(act, down[...])

    @pl.when(step == 0)
    def _():
        acc[...] = part

    @pl.when(step > 0)
    def _():
        acc[...] += part

    @pl.when(step == pl.num_programs(0) - 1)
    def _():
        share = own_ref.shape[0]
        ffn_ref[...] = acc[...].astype(BF16)
        mine = pl.ds(pl.multiple_of(at_ref[0] * share, share), share)
        own_ref[...] = acc[mine, :] + emb_ref[mine, :].astype(F32)


def encode(y, emb, weights, share, tiles):
    count, width = emb.shape
    hidden = weights[0].shape[0]
    tile = hidden // tiles
    return call(
        encode_kernel,
        (tiles,),
        y.reshape(1),
        [(emb, emb.shape, whole_block(2))]
        + [(w, (tile, width), lambda i, at: (i, 0)) for w in weights],
        [
            (shape((count, width), BF16), (count, width), whole_block(2)),
            (shape((share, width), F32), (share, width), whole_block(2)),
        ],
        [pltpu.VMEM((count, width), BF16), pltpu.VMEM((count, width), F32)],
    )


def span_rows(halves, g, cols):
    parts = [half[:, g, :, cols] for half in halves]
    parts = [p.reshape(p.shape[0] * p.shape[1], p.shape[2]) for p in parts]
    return jnp.concatenate(parts, axis=0)


def attend_kernel(span, head_dim, turn, at_ref, q_ref, k_ref, v_ref, k2_ref, v2_ref, attn_ref, prob_ref, stage):
    blocks, groups, piece, inner = k_ref.shape
    heads, keys_per = inner // head_dim, 2 * blocks * piece
    nlen = keys_per // 2
    scale = head_dim ** (-0.5)
    toks = attn_ref.shape[0]
    lane = lax.broadcasted_iota(jnp.int32, (span, keys_per), 1)
    key = lane
    for i in range(2 * blocks):
        start = at_ref[2 * groups * 3 + i]
        here = jnp.logical_and(lane >= i * piece, lane < (i + 1) * piece)
        key = jnp.where(here, lane + (start - i * piece), key)
    for g in range(groups):
        rows = pl.ds(g * span, span)
        for h in range(heads):
            cols = pl.ds(h * head_dim, head_dim)
            prob_ref[h, rows, :] = dot_t(q_ref[0, rows, cols], span_rows((k_ref, k2_ref), g, cols))
    for g in range(groups):
        rows = pl.ds(g * span, span)
        base = (turn * groups + g) * 3
        first, second, live = at_ref[base], at_ref[base + 1], at_ref[base + 2]
        mask = jnp.logical_or(key < first, jnp.logical_and(key >= nlen, key < nlen + second))
        weight = live.astype(F32)
        for h in range(heads):
            cols = pl.ds(h * head_dim, head_dim)
            expo = jnp.where(mask, jnp.exp(prob_ref[h, rows, :] * scale), 0.0)
            prob = expo * (weight / jnp.sum(expo, axis=-1, keepdims=True))
            prob_ref[h, rows, :] = prob
            stage[rows, cols] = dot(prob.astype(BF16), span_rows((v_ref, v2_ref), g, cols))
    attn_ref[...] = stage[1 : toks + 1, :].astype(BF16)


def backward_kernel(
    span, head_dim, turn, at_ref, prob_ref, d_ref, k_ref, v_ref, k2_ref, v2_ref, dq_ref, stage, d_prob
):
    groups, inner = k_ref.shape[1], k_ref.shape[3]
    heads = inner // head_dim
    scale = head_dim ** (-0.5)
    toks = dq_ref.shape[0]
    for g in range(groups):
        rows = pl.ds(g * span, span)
        for h in range(heads):
            cols = pl.ds(h * head_dim, head_dim)
            d_prob[h, rows, :] = dot_t(d_ref[0, rows, cols], span_rows((v_ref, v2_ref), g, cols))
    for g in range(groups):
        rows = pl.ds(g * span, span)
        for h in range(heads):
            cols = pl.ds(h * head_dim, head_dim)
            prob, slope = prob_ref[h, rows, :], d_prob[h, rows, :]
            delta = jnp.sum(prob * slope, axis=-1, keepdims=True)
            d_score = (prob * (slope - delta) * scale).astype(BF16)
            stage[rows, cols] = dot(d_score, span_rows((k_ref, k2_ref), g, cols))
    dq_ref[...] = stage[1 : toks + 1, :].astype(BF16)


def over_shard(kernel, turn, at, padded, kv, span, head_dim, prob):
    _, rows, inner = padded.shape
    toks, heads = rows - span, inner // head_dim
    probs = shape((heads, rows, 2 * kv[0].shape[0] * kv[0].shape[2]), F32)
    operands = [(padded, (1, rows, inner), lambda i, at: (turn, 0, 0))]
    operands += [(a, a.shape, whole_block(4)) for a in kv]
    outs = [(shape((toks, inner), BF16), (toks, inner), whole_block(2))]
    scratch = [pltpu.VMEM((rows, inner), F32)]
    if prob is None:
        outs.append((probs, probs.shape, whole_block(3)))
    else:
        operands.insert(0, (prob, prob.shape, whole_block(3)))
        scratch.append(pltpu.VMEM(probs.shape, F32))
    return call(functools.partial(kernel, span, head_dim, turn), (1,), at, operands, outs, scratch)


def sent_kernel(at_ref, own_ref, other_ref, w_ref, out_ref):
    rows = jnp.concatenate([own_ref[...], other_ref[...]], axis=0)
    out_ref[0] = dot_t(rows, w_ref[...]).astype(BF16)


def kept_kernel(at_ref, own_rows_ref, other_rows_ref, w_ref, add_ref, both_ref, y_ref, zl_ref, own_ref):
    def total(rows_ref, start):
        add = add_ref[0, start : start + rows_ref.shape[0], :]
        return dot_t(rows_ref[...], w_ref[...]) + add.astype(F32)

    @pl.when(pl.program_id(0) == 0)
    def _():
        y_ref[...] = total(own_rows_ref, 0).astype(BF16)
        both_ref[...] = total(other_rows_ref, own_ref.shape[0]).astype(BF16)

    @pl.when(pl.program_id(0) == 1)
    def _():
        own_ref[...] = total(own_rows_ref, 0)
        zl_ref[...] = total(other_rows_ref, own_ref.shape[0]).astype(BF16)


def columns(at, rows, w, wm, add=None):
    toks, inner = rows[0].shape
    operands = [(a, a.shape, whole_block(2)) for a in rows]
    operands.append((w, (wm, inner), lambda i, at: (at[i], 0)))
    moved = (1, 2 * toks, wm), lambda i, at: (i, 0, 0)
    if add is None:
        out = shape((2, 2 * toks, wm), BF16)
        return call(sent_kernel, (2,), at, operands, [(out,) + moved], [])[0]
    operands.append((add,) + moved)
    outs = [(shape((toks, wm), dtype), (toks, wm), whole_block(2)) for dtype in (BF16, BF16, BF16, F32)]
    return call(kept_kernel, (2,), at, operands, outs, [])


def core_sums(rows, w):
    y, c = lax.axis_index("y"), lax.axis_index("c")
    ny = lax.axis_size("y")
    wm = w.shape[0] // (2 * ny)
    if ny != 2:
        return None
    return columns(jnp.stack([(1 - y) * 2 + (1 - c), y * 2 + (1 - c)]), rows, w, wm)


def sum_heads(rows, w, sent):
    zl, y, c = (lax.axis_index(name) for name in GROUP)
    ny = lax.axis_size("y")
    wm = w.shape[0] // (2 * ny)
    if ny != 2:
        rows = jnp.concatenate(rows, axis=0)
        count = rows.shape[0]
        rows = jnp.roll(rows, zl * (count // 2), axis=0)
        blocks = dot_t(rows, w).astype(BF16).reshape(2, count // 2, ny, 2, wm)
        blocks = blocks.transpose(0, 2, 3, 1, 4).reshape(ny * 2 * count, wm)
        return lax.psum_scatter(blocks, GROUP, scatter_dimension=0, tiled=True).astype(BF16), (), ()
    at = jnp.stack([(1 - y) * 2 + c, y * 2 + c])
    to_both, to_y, to_zl, own = columns(at, rows, w, wm, flip(sent, "c"))
    over_both = lax.ppermute(to_both, ("zl", "y"), [(i, 3 - i) for i in range(4)])
    over_y, over_zl = flip(to_y, "y"), flip(to_zl, "zl")
    total = own + over_zl.astype(F32) + over_y.astype(F32) + over_both.astype(F32)
    return total.astype(BF16), (to_both, to_y, to_zl), (over_both, over_y, over_zl)


def per_device(
    hidden,
    cotangent,
    neighbour_ids,
    neighbour_lengths,
    embed_table,
    enc_up,
    enc_down,
    w_query,
    w_keyval,
    w_out,
):
    zh, zl, x = (lax.axis_index(name) for name in SEQ)
    y, c = lax.axis_index("y"), lax.axis_index("c")
    nzh, ny = lax.axis_size("zh"), lax.axis_size("y")
    spans_here, neigh, nlen = neighbour_ids.shape
    toks = hidden.shape[0]
    span = toks // spans_here
    keys_per = neigh * nlen
    groups = spans_here + 1
    rows_here, heads_here, head_dim = w_query.shape
    heads = heads_here // 2
    inner = heads * head_dim
    kv_rows, enc_width = w_keyval.shape[0], embed_table.shape[1]
    seqs = 4 * nzh
    piece = keys_per // (2 * ny)

    qkv_rows = rows_here + 2 * kv_rows

    def shard_at(hop, at_zl, at_x):
        return (lax.rem(zh + (nzh - hop), nzh) * 2 + at_zl) * 2 + at_x

    packed = pack(zl, w_query, w_keyval, w_out, hidden, cotangent)
    other_qkv, other_out, own, own_q, own_kv, own_out, states = packed
    up2, down2 = flip(enc_up, "c"), flip(enc_down, "c")
    beside_qkv = flip(other_qkv, "zl")
    own_x = flip(own, "x")
    hop_q = onward(own_q, "zh")

    def gather_states(rows):
        return lax.all_gather(rows, ("y", "c"), axis=0, tiled=False)

    own_states = gather_states(states)

    ids = neighbour_ids.reshape(spans_here, 2, ny, piece).transpose(1, 2, 0, 3).reshape(-1)
    vocab_here = embed_table.shape[0]
    local_ids = tie(ids, other_qkv) - (y * 2 + c) * vocab_here
    inside = jnp.logical_and(local_ids >= 0, local_ids < vocab_here)
    clipped = jnp.clip(local_ids, 0, vocab_here - 1)
    picked = tie(embed_table.at[clipped].get(mode="promise_in_bounds"), hop_q, beside_qkv, up2, down2)
    half_rows = ids.shape[0] // 2

    def half_emb(core):
        rows = lax.dynamic_slice_in_dim(picked, core * half_rows, half_rows, 0)
        live = lax.dynamic_slice_in_dim(inside, core * half_rows, half_rows, 0)
        return jnp.where(live[:, None], rows, jnp.zeros((), BF16))

    emb_other = half_emb(1 - c)
    emb = tie(half_emb(c), own_x) + flip(emb_other, "c")

    beside_qkv, other_out, hop_q = (tie(a, emb) for a in (beside_qkv, other_out, hop_q))
    beside_qkv_x, hop_q_x = flip(beside_qkv, "x"), flip(hop_q, "x")
    hop_q2 = onward(beside_qkv[:rows_here], "zh")
    beside_out = flip(other_out, "zl")
    emb = emb + flip(emb, "y") if ny == 2 else lax.psum(emb, "y")
    emb = tie(emb, beside_qkv_x, hop_q_x, hop_q2, beside_out, own_states)

    own_kv, beside_out, states = (tie(a, emb) for a in (own_kv, beside_out, states))
    hop_kv = onward(own_kv, "zh")
    beside_out_x = flip(beside_out, "x")
    other_states = flip(states, "zl")
    share_rows = half_rows // ny
    ffn, share = encode(y, emb, [enc_up, enc_down, up2, down2], share_rows, 2)
    ffn = tie(ffn, hop_kv)
    hop_kv2 = onward(tie(beside_qkv, ffn)[rows_here:], "zh")
    if ny == 2:
        sent = lax.dynamic_slice_in_dim(ffn, (1 - y) * share_rows, share_rows, 0)
        share = share + flip(sent, "y").astype(F32)
    else:
        share = lax.psum_scatter(ffn, "y", scatter_dimension=0, tiled=True).astype(F32)
        share = share + lax.dynamic_slice_in_dim(emb, y * share_rows, share_rows, 0).astype(F32)
    encoded = rms_rows(tie(share, beside_out_x, other_states, hop_kv2)).astype(BF16)

    other_states = gather_states(tie(other_states, encoded))
    before = lax.ppermute(encoded[share_rows - piece :], SEQ, [(i, i + 1) for i in range(seqs - 1)])
    encoded = jnp.concatenate([before, encoded], axis=0)
    hop_qkv = jnp.concatenate([tie(hop_q2, encoded), hop_kv, hop_kv2], axis=0)
    hop_qkv_x = flip(hop_qkv, "x")
    hop_out = onward(jnp.concatenate([tie(own_out, encoded), beside_out], axis=0), "zh")

    if ny == 2:
        corner = lax.ppermute(encoded, ("zl", "y"), [(i, 3 - i) for i in range(4)])
        over_y, over_zl = flip(encoded, "y"), flip(encoded, "zl")
        over_y = tie(over_y, hop_qkv_x)
        own_rows, other_rows = [encoded, over_y], [over_zl, corner]
        ys = [y, 1 - y]
    else:
        own_rows = [lax.all_gather(encoded, "y", axis=0, tiled=True)]
        other_rows, over_y = [flip(own_rows[0], "zl")], own_rows[0]
        ys = [jnp.int32(i) for i in range(ny)]

    q_pieces, kv_pieces, out_pieces = [], [], []

    def add_kv(at, block, start):
        kv_pieces.append((at, block, start, kv_rows, 0))
        kv_pieces.append((at, block, start + kv_rows, kv_rows, 1))

    here, here_x = shard_at(0, zl, x), shard_at(0, zl, 1 - x)
    there, there_x = shard_at(0, 1 - zl, x), shard_at(0, 1 - zl, 1 - x)
    for at, block, start in ((here, own_q, 0), (here_x, own_x, 0), (there, beside_qkv, 0), (there_x, beside_qkv_x, 0)):
        q_pieces.append((at, block, start, rows_here, None))
    for at, block, start in (
        (here, own_kv, 0),
        (here_x, own_x, rows_here),
        (there, beside_qkv, rows_here),
        (there_x, beside_qkv_x, rows_here),
    ):
        add_kv(at, block, start)
    for at, block, start in ((here, own_out, 0), (here_x, own_x, qkv_rows), (there, beside_out, 0), (there_x, beside_out_x, 0)):
        out_pieces.append((at, block, start, rows_here, None))
    for hop in range(1, nzh):
        if hop > 1:
            hop_q, hop_qkv = onward(hop_q, "zh"), onward(hop_qkv, "zh")
            hop_q_x, hop_qkv_x = flip(hop_q, "x"), flip(hop_qkv, "x")
        for at_x, at_q, at_qkv in ((x, hop_q, hop_qkv), (1 - x, hop_q_x, hop_qkv_x)):
            here, there = shard_at(hop, zl, at_x), shard_at(hop, 1 - zl, at_x)
            q_pieces += [(here, at_q, 0, rows_here, None), (there, at_qkv, 0, rows_here, None)]
            add_kv(here, at_qkv, rows_here)
            add_kv(there, at_qkv, qkv_rows)

    lens_pad = jnp.concatenate([jnp.ones((1, neigh), jnp.int32), neighbour_lengths], axis=0)
    at = []
    for turn in range(2):
        first = ((zh * 2 + lax.rem(zl + turn, 2)) * 2 + x) * spans_here
        rows = lax.dynamic_slice_in_dim(lens_pad, first, groups, 0)
        live = (first + jnp.arange(groups, dtype=jnp.int32) > 0).astype(jnp.int32)
        at.append(jnp.concatenate([rows, live[:, None]], axis=1).reshape(-1))
    starts = [(core * ny + at_y) * piece for core in (c, 1 - c) for at_y in ys]
    at = jnp.concatenate(at + [jnp.stack(starts).astype(jnp.int32)])

    w_dims = (seqs * rows_here, inner)
    q_pieces[0] = (q_pieces[0][0], tie(q_pieces[0][1], over_y)) + q_pieces[0][2:]
    kv_pieces[0] = (kv_pieces[0][0], tie(kv_pieces[0][1], over_y)) + kv_pieces[0][2:]
    wkv = place(kv_pieces, (2, enc_width, inner))
    wq, wo = place(q_pieces, w_dims), place(out_pieces, w_dims)
    every = jnp.arange(2 * ny, dtype=jnp.int32)
    kv_shape = (ny, groups, piece, inner)
    states = (own_states, other_states)

    def at_of(pieces):
        return jnp.stack([p[0] for p in pieces])

    def keys_values(rows, rows2):
        near = keyval(at, rows, wkv)
        far = keyval(at, tie(rows2, *near), wkv)
        return [a.reshape(kv_shape) for a in (*near, *far)]

    def attend(turn, kv, query):
        return over_shard(attend_kernel, turn, at, query, kv, span, head_dim, None)

    own_rows = jnp.concatenate(own_rows, axis=0)
    own_rows2 = flip(own_rows, "c")
    kv = keys_values(own_rows, own_rows2)
    query = project(every, states, 0, tie(wq, wo, *kv), hidden.shape[1], span, True)
    attn, prob = attend(0, kv, query)
    other_rows = jnp.concatenate(lax.optimization_barrier((*other_rows, attn))[:-1], axis=0)
    other_rows2 = flip(other_rows, "c")
    hop_out = tie(hop_out, attn)
    hop_out_x = flip(hop_out, "x")
    kv2 = keys_values(other_rows, other_rows2)
    attn2, prob2 = attend(1, kv2, query)
    some = project(at_of(out_pieces), states, 1, tie(wo, attn2), rows_here, span, False)

    late = []
    for hop in range(1, nzh):
        if hop > 1:
            hop_out = onward(hop_out, "zh")
            hop_out_x = flip(hop_out, "x")
        for at_x, block in ((x, hop_out), (1 - x, hop_out_x)):
            late.append((shard_at(hop, zl, at_x), block, 0, rows_here, None))
            late.append((shard_at(hop, 1 - zl, at_x), block, rows_here, rows_here, None))

    hop_out_x = tie(hop_out_x, some)
    late[-2:] = [(p[0], hop_out_x) + p[2:] for p in late[-2:]]
    wo = place(late, w_dims, wo)
    attn = (attn, attn2)
    out_sent = core_sums(attn, wo)
    if out_sent is not None:
        some = tie(some, out_sent)
    d_attn = project(at_of(late), states, 1, wo, rows_here, span, True, some)
    cca_out, moved, arrived = sum_heads((attn[0], tie(attn[1], d_attn)), wo, out_sent)
    d_attn = tie(d_attn, *moved)
    d_query = [
        over_shard(backward_kernel, turn, at, d_attn, kv_here, span, head_dim, prob_here)[0]
        for turn, kv_here, prob_here in ((0, kv, prob), (1, kv2, prob2))
    ]
    grad_sent = core_sums(d_query, wq)
    if arrived:
        grad_sent = tie(grad_sent, *arrived)
    hidden_grad, _, _ = sum_heads(d_query, wq, grad_sent)
    return (cca_out, hidden_grad)


def solution(mesh):
    ns, nm = mesh.shape["seq"], mesh.shape["mp"]
    fine = Mesh(mesh.devices.reshape(ns // 4, 2, 2, nm // 2, 2), ("zh", "zl", "x", "y", "c"))
    seq, mp = SEQ, ("y", "c")
    return jax.shard_map(
        per_device,
        mesh=fine,
        in_specs=(
            P(seq, mp),
            P(seq, mp),
            P(seq, None, None),
            P(),
            P(mp, None),
            P(mp, None),
            P(mp, None),
            P(seq, mp, None),
            P(seq, mp, None, None),
            P(seq, mp, None),
        ),
        out_specs=(P(seq, mp), P(seq, mp)),
        check_vma=False,
    )
```

```python
import functools

import jax
import jax.numpy as jnp
from jax import lax
from jax.experimental import pallas as pl
from jax.experimental.pallas import tpu as pltpu
from jax.sharding import Mesh
from jax.sharding import PartitionSpec as P

SEQ = ("zh", "zl", "x")
GROUP = ("zl", "y", "c")
VMEM = 62 * 1024 * 1024
F32 = jnp.float32
BF16 = jnp.bfloat16


def flip(shard, axis):
    return lax.ppermute(shard, axis, [(0, 1), (1, 0)])


def onward(shard, axis):
    count = lax.axis_size(axis)
    return lax.ppermute(shard, axis, [(i, (i + 1) % count) for i in range(count)])


def tie(value, *earlier):
    return lax.optimization_barrier((value,) + earlier)[0]


def rms_rows(values):
    return values * lax.rsqrt(jnp.mean(values * values, axis=-1, keepdims=True) + 1e-06)


def dot(left, right):
    return jnp.dot(left, right, preferred_element_type=F32)


def dot_t(left, right):
    return lax.dot_general(left, right, (((1,), (1,)), ((), ())), preferred_element_type=F32)


def call(kernel, grid, prefetch, operands, outs, scratch):
    arrays = [o[0] for o in operands]
    return pl.pallas_call(
        kernel,
        grid_spec=pltpu.PrefetchScalarGridSpec(
            num_scalar_prefetch=1,
            grid=grid,
            in_specs=[pl.BlockSpec(block, index) for _, block, index in operands],
            out_specs=[pl.BlockSpec(block, index) for _, block, index in outs],
            scratch_shapes=scratch,
        ),
        out_shape=[o[0] for o in outs],
        compiler_params=pltpu.CompilerParams(vmem_limit_bytes=VMEM),
        cost_estimate=pl.CostEstimate(flops=20000000000, bytes_accessed=1, transcendentals=0),
    )(prefetch, *arrays)


def shape(dims, dtype):
    return jax.ShapeDtypeStruct(dims, dtype)


def whole_block(ndim):
    return lambda *_: (0,) * ndim


def pack_kernel(
    at_ref, q_ref, kv_ref, o_ref, h_ref, c_ref,
    other_qkv_ref, other_out_ref, own_ref, own_q_ref, own_kv_ref, own_out_ref, states_ref,
    q, kv, o,
):
    rows, inner = own_out_ref.shape
    kv_rows, heads, _, head_dim = kv_ref.shape
    q[...] = q_ref[...].reshape(q.shape)
    o[...] = o_ref[...].reshape(o.shape)
    kv[...] = kv_ref[...].reshape(kv.shape)

    def cut(of, start, size):
        return of[:, pl.ds(pl.multiple_of(start, head_dim), size)]

    def copy(which, q_dst, kv_dst, out_dst):
        q_dst[...] = cut(q, which * inner, inner)
        out_dst[...] = cut(o, which * inner, inner)
        for h in range(heads // 2):
            for i in range(2):
                piece = cut(kv, ((which * (heads // 2) + h) * 2 + i) * head_dim, head_dim)
                kv_dst[i * kv_rows : (i + 1) * kv_rows, h * head_dim : (h + 1) * head_dim] = piece

    zl = at_ref[0]
    kv_end = rows + 2 * kv_rows
    copy(1 - zl, other_qkv_ref.at[:rows], other_qkv_ref.at[rows:], other_out_ref)
    copy(zl, own_ref.at[:rows], own_ref.at[rows:kv_end], own_ref.at[kv_end:])
    copy(zl, own_q_ref, own_kv_ref, own_out_ref)
    states_ref[0] = h_ref[...]
    states_ref[1] = c_ref[...]


def pack(zl, w_query, w_keyval, w_out, hidden, cotangent):
    rows, heads, head_dim = w_query.shape
    kv_rows, inner = w_keyval.shape[0], heads // 2 * head_dim
    sizes = [rows + 2 * kv_rows, rows, 2 * rows + 2 * kv_rows, rows, 2 * kv_rows, rows]
    outs = [(n, inner) for n in sizes] + [(2,) + hidden.shape]
    return call(
        pack_kernel,
        (1,),
        zl.reshape(1),
        [(a, a.shape, whole_block(a.ndim)) for a in (w_query, w_keyval, w_out, hidden, cotangent)],
        [(shape(dims, BF16), dims, whole_block(len(dims))) for dims in outs],
        [pltpu.VMEM(dims, BF16) for dims in ((rows, 2 * inner), (kv_rows, 4 * inner), (rows, 2 * inner))],
    )


def place_kernel(jobs, count, through, at_ref, *refs):
    sources, out_ref, sems = refs[:count], refs[count + through], refs[-1]
    stage = refs[-2] if through else out_ref

    def dst(ref, i, rows, plane):
        to = pl.ds(pl.multiple_of(at_ref[i] * rows, 16), rows)
        return ref.at[to] if plane is None else ref.at[plane, to]

    copies = []
    for i, (source, start, rows, plane) in enumerate(jobs):
        src = sources[source].at[pl.ds(start, rows)]
        to = stage.at[pl.ds(i * rows, rows)] if through else dst(stage, i, rows, plane)
        copies.append(pltpu.make_async_copy(src, to, sems.at[i]))
    for copy in copies:
        copy.start()
    for copy in copies:
        copy.wait()
    if through:
        copies = []
        for i, (_, _, rows, plane) in enumerate(jobs):
            src = stage.at[pl.ds(i * rows, rows)]
            copies.append(pltpu.make_async_copy(src, dst(out_ref, i, rows, plane), sems.at[i]))
        for copy in copies:
            copy.start()
        for copy in copies:
            copy.wait()


def place(pieces, dims, base=None):
    sources = []
    for piece in pieces:
        if not any(piece[1] is a for a in sources):
            sources.append(piece[1])
    index = [next(i for i, a in enumerate(sources) if a is piece[1]) for piece in pieces]
    jobs = [(i, p[2], p[3], p[4]) for i, p in zip(index, pieces)]
    if any(rows % 16 for _, _, rows, _ in jobs):
        whole = jnp.zeros(dims, BF16) if base is None else base
        for (at, block, start, rows, plane) in pieces:
            block = block[start : start + rows]
            if plane is None:
                whole = lax.dynamic_update_slice(whole, block, (at * rows, 0))
            else:
                whole = lax.dynamic_update_slice(whole, block[None], (plane, at * rows, 0))
        return whole
    through = base is not None
    arrays = sources + [base] if through else sources
    scratch = [pltpu.SemaphoreType.DMA((len(jobs),))]
    if through:
        scratch.insert(0, pltpu.VMEM((len(jobs) * jobs[0][2], dims[-1]), BF16))
    out_spec = pl.BlockSpec(memory_space=pl.ANY) if through else pl.BlockSpec(dims, whole_block(len(dims)))
    return pl.pallas_call(
        functools.partial(place_kernel, jobs, len(sources), int(through)),
        grid_spec=pltpu.PrefetchScalarGridSpec(
            num_scalar_prefetch=1,
            grid=(1,),
            in_specs=[pl.BlockSpec(memory_space=pl.ANY)] * len(arrays),
            out_specs=out_spec,
            scratch_shapes=scratch,
        ),
        out_shape=shape(dims, BF16),
        input_output_aliases={len(arrays): 0} if through else {},
        compiler_params=pltpu.CompilerParams(vmem_limit_bytes=VMEM),
        cost_estimate=pl.CostEstimate(flops=20000000000, bytes_accessed=1, transcendentals=0),
    )(jnp.stack([p[0] for p in pieces]).astype(jnp.int32), *arrays)


def project_kernel(span, first, last, at_ref, own_ref, other_ref, w_ref, *rest):
    out_ref, acc = rest[-2:]
    step = pl.program_id(0)
    toks, cols = own_ref.shape[0], acc.shape[1]
    rows = jnp.concatenate([own_ref[...], other_ref[...]], axis=0)
    part = dot(rows, w_ref[...])

    @pl.when(step == 0)
    def _():
        acc[...] = part if first else part + rest[0][...]

    @pl.when(step > 0)
    def _():
        acc[...] += part

    @pl.when(step == pl.num_programs(0) - 1)
    def _():
        if not last:
            out_ref[...] = acc[...]
            return
        front, back = jnp.zeros((1, cols), F32), jnp.zeros((span - 1, cols), F32)
        for s in range(2):
            own = acc[s * toks : (s + 1) * toks, :]
            out_ref[s] = jnp.concatenate([front, own, back], axis=0).astype(BF16)


def project(at, states, which, w, wide, span, last, before=None):
    toks, wm = states[0].shape[2:]
    cols, steps, per = w.shape[1], at.shape[0], wm // wide
    operands = [
        (a, (None, None, toks, wide), lambda i, at: (at[i] // per, which, 0, lax.rem(at[i], per)))
        for a in states
    ]
    operands += [
        (w, (wide, cols), lambda i, at: (at[i], 0)),
    ]
    total = (2 * toks, cols)
    if before is not None:
        operands.append((before, total, whole_block(2)))
    out = shape((2, toks + span, cols), BF16) if last else shape(total, F32)
    return call(
        functools.partial(project_kernel, span, before is None, last),
        (steps,),
        at,
        operands,
        [(out, out.shape, whole_block(len(out.shape)))],
        [pltpu.VMEM(total, F32)],
    )[0]


def keyval_kernel(at_ref, rows_ref, w_ref, k_ref, v_ref):
    rows = rows_ref[...]
    k_ref[...] = dot(rows, w_ref[0]).astype(BF16)
    v_ref[...] = dot(rows, w_ref[1]).astype(BF16)


def keyval(at, rows, w):
    out = shape((rows.shape[0], w.shape[2]), BF16)
    operands = [(a, a.shape, whole_block(a.ndim)) for a in (rows, w)]
    return call(keyval_kernel, (1,), at, operands, [(out, out.shape, whole_block(2))] * 2, [])


def encode_kernel(at_ref, emb_ref, up_ref, down_ref, up2_ref, down2_ref, ffn_ref, own_ref, normed, acc):
    step = pl.program_id(0)

    @pl.when(step == 0)
    def _():
        normed[...] = rms_rows(emb_ref[...].astype(F32)).astype(BF16)

    part = 0.0
    for up, down in ((up_ref, down_ref), (up2_ref, down2_ref)):
        act = jax.nn.gelu(dot_t(normed[...], up[...])).astype(BF16)
        part = part + dot(act, down[...])

    @pl.when(step == 0)
    def _():
        acc[...] = part

    @pl.when(step > 0)
    def _():
        acc[...] += part

    @pl.when(step == pl.num_programs(0) - 1)
    def _():
        share = own_ref.shape[0]
        ffn_ref[...] = acc[...].astype(BF16)
        mine = pl.ds(pl.multiple_of(at_ref[0] * share, share), share)
        own_ref[...] = acc[mine, :] + emb_ref[mine, :].astype(F32)


def encode(y, emb, weights, share, tiles):
    count, width = emb.shape
    hidden = weights[0].shape[0]
    tile = hidden // tiles
    return call(
        encode_kernel,
        (tiles,),
        y.reshape(1),
        [(emb, emb.shape, whole_block(2))]
        + [(w, (tile, width), lambda i, at: (i, 0)) for w in weights],
        [
            (shape((count, width), BF16), (count, width), whole_block(2)),
            (shape((share, width), F32), (share, width), whole_block(2)),
        ],
        [pltpu.VMEM((count, width), BF16), pltpu.VMEM((count, width), F32)],
    )


def span_rows(halves, g, cols):
    parts = [half[:, g, :, cols] for half in halves]
    parts = [p.reshape(p.shape[0] * p.shape[1], p.shape[2]) for p in parts]
    return jnp.concatenate(parts, axis=0)


def attend_kernel(span, head_dim, turn, at_ref, q_ref, k_ref, v_ref, k2_ref, v2_ref, attn_ref, prob_ref, stage):
    blocks, groups, piece, inner = k_ref.shape
    heads, keys_per = inner // head_dim, 2 * blocks * piece
    nlen = keys_per // 2
    scale = head_dim ** (-0.5)
    toks = attn_ref.shape[0]
    lane = lax.broadcasted_iota(jnp.int32, (span, keys_per), 1)
    key = lane
    for i in range(2 * blocks):
        start = at_ref[2 * groups * 3 + i]
        here = jnp.logical_and(lane >= i * piece, lane < (i + 1) * piece)
        key = jnp.where(here, lane + (start - i * piece), key)
    for g in range(groups):
        rows = pl.ds(g * span, span)
        for h in range(heads):
            cols = pl.ds(h * head_dim, head_dim)
            prob_ref[h, rows, :] = dot_t(q_ref[0, rows, cols], span_rows((k_ref, k2_ref), g, cols))
    for g in range(groups):
        rows = pl.ds(g * span, span)
        base = (turn * groups + g) * 3
        first, second, live = at_ref[base], at_ref[base + 1], at_ref[base + 2]
        mask = jnp.logical_or(key < first, jnp.logical_and(key >= nlen, key < nlen + second))
        weight = live.astype(F32)
        for h in range(heads):
            cols = pl.ds(h * head_dim, head_dim)
            expo = jnp.where(mask, jnp.exp(prob_ref[h, rows, :] * scale), 0.0)
            prob = expo * (weight / jnp.sum(expo, axis=-1, keepdims=True))
            prob_ref[h, rows, :] = prob
            stage[rows, cols] = dot(prob.astype(BF16), span_rows((v_ref, v2_ref), g, cols))
    attn_ref[...] = stage[1 : toks + 1, :].astype(BF16)


def backward_kernel(
    span, head_dim, turn, at_ref, prob_ref, d_ref, k_ref, v_ref, k2_ref, v2_ref, dq_ref, stage, d_prob
):
    groups, inner = k_ref.shape[1], k_ref.shape[3]
    heads = inner // head_dim
    scale = head_dim ** (-0.5)
    toks = dq_ref.shape[0]
    for g in range(groups):
        rows = pl.ds(g * span, span)
        for h in range(heads):
            cols = pl.ds(h * head_dim, head_dim)
            d_prob[h, rows, :] = dot_t(d_ref[0, rows, cols], span_rows((v_ref, v2_ref), g, cols))
    for g in range(groups):
        rows = pl.ds(g * span, span)
        for h in range(heads):
            cols = pl.ds(h * head_dim, head_dim)
            prob, slope = prob_ref[h, rows, :], d_prob[h, rows, :]
            delta = jnp.sum(prob * slope, axis=-1, keepdims=True)
            d_score = (prob * (slope - delta) * scale).astype(BF16)
            stage[rows, cols] = dot(d_score, span_rows((k_ref, k2_ref), g, cols))
    dq_ref[...] = stage[1 : toks + 1, :].astype(BF16)


def over_shard(kernel, turn, at, padded, kv, span, head_dim, prob):
    _, rows, inner = padded.shape
    toks, heads = rows - span, inner // head_dim
    probs = shape((heads, rows, 2 * kv[0].shape[0] * kv[0].shape[2]), F32)
    operands = [(padded, (1, rows, inner), lambda i, at: (turn, 0, 0))]
    operands += [(a, a.shape, whole_block(4)) for a in kv]
    outs = [(shape((toks, inner), BF16), (toks, inner), whole_block(2))]
    scratch = [pltpu.VMEM((rows, inner), F32)]
    if prob is None:
        outs.append((probs, probs.shape, whole_block(3)))
    else:
        operands.insert(0, (prob, prob.shape, whole_block(3)))
        scratch.append(pltpu.VMEM(probs.shape, F32))
    return call(functools.partial(kernel, span, head_dim, turn), (1,), at, operands, outs, scratch)


def sent_kernel(at_ref, own_ref, other_ref, w_ref, out_ref):
    rows = jnp.concatenate([own_ref[...], other_ref[...]], axis=0)
    out_ref[0] = dot_t(rows, w_ref[...]).astype(BF16)


def kept_kernel(at_ref, own_rows_ref, other_rows_ref, w_ref, add_ref, both_ref, y_ref, zl_ref, own_ref):
    def total(rows_ref, start):
        add = add_ref[0, start : start + rows_ref.shape[0], :]
        return dot_t(rows_ref[...], w_ref[...]) + add.astype(F32)

    @pl.when(pl.program_id(0) == 0)
    def _():
        y_ref[...] = total(own_rows_ref, 0).astype(BF16)
        both_ref[...] = total(other_rows_ref, own_ref.shape[0]).astype(BF16)

    @pl.when(pl.program_id(0) == 1)
    def _():
        own_ref[...] = total(own_rows_ref, 0)
        zl_ref[...] = total(other_rows_ref, own_ref.shape[0]).astype(BF16)


def columns(at, rows, w, wm, add=None):
    toks, inner = rows[0].shape
    operands = [(a, a.shape, whole_block(2)) for a in rows]
    operands.append((w, (wm, inner), lambda i, at: (at[i], 0)))
    moved = (1, 2 * toks, wm), lambda i, at: (i, 0, 0)
    if add is None:
        out = shape((2, 2 * toks, wm), BF16)
        return call(sent_kernel, (2,), at, operands, [(out,) + moved], [])[0]
    operands.append((add,) + moved)
    outs = [(shape((toks, wm), dtype), (toks, wm), whole_block(2)) for dtype in (BF16, BF16, BF16, F32)]
    return call(kept_kernel, (2,), at, operands, outs, [])


def core_sums(rows, w):
    y, c = lax.axis_index("y"), lax.axis_index("c")
    ny = lax.axis_size("y")
    wm = w.shape[0] // (2 * ny)
    if ny != 2:
        return None
    return columns(jnp.stack([(1 - y) * 2 + (1 - c), y * 2 + (1 - c)]), rows, w, wm)


def sum_heads(rows, w, sent):
    zl, y, c = (lax.axis_index(name) for name in GROUP)
    ny = lax.axis_size("y")
    wm = w.shape[0] // (2 * ny)
    if ny != 2:
        rows = jnp.concatenate(rows, axis=0)
        count = rows.shape[0]
        rows = jnp.roll(rows, zl * (count // 2), axis=0)
        blocks = dot_t(rows, w).astype(BF16).reshape(2, count // 2, ny, 2, wm)
        blocks = blocks.transpose(0, 2, 3, 1, 4).reshape(ny * 2 * count, wm)
        return lax.psum_scatter(blocks, GROUP, scatter_dimension=0, tiled=True).astype(BF16), (), ()
    at = jnp.stack([(1 - y) * 2 + c, y * 2 + c])
    to_both, to_y, to_zl, own = columns(at, rows, w, wm, flip(sent, "c"))
    over_both = lax.ppermute(to_both, ("zl", "y"), [(i, 3 - i) for i in range(4)])
    over_y, over_zl = flip(to_y, "y"), flip(to_zl, "zl")
    total = own + over_zl.astype(F32) + over_y.astype(F32) + over_both.astype(F32)
    return total.astype(BF16), (to_both, to_y, to_zl), (over_both, over_y, over_zl)


def per_device(
    hidden,
    cotangent,
    neighbour_ids,
    neighbour_lengths,
    embed_table,
    enc_up,
    enc_down,
    w_query,
    w_keyval,
    w_out,
):
    zh, zl, x = (lax.axis_index(name) for name in SEQ)
    y, c = lax.axis_index("y"), lax.axis_index("c")
    nzh, ny = lax.axis_size("zh"), lax.axis_size("y")
    spans_here, neigh, nlen = neighbour_ids.shape
    toks = hidden.shape[0]
    span = toks // spans_here
    keys_per = neigh * nlen
    groups = spans_here + 1
    rows_here, heads_here, head_dim = w_query.shape
    heads = heads_here // 2
    inner = heads * head_dim
    kv_rows, enc_width = w_keyval.shape[0], embed_table.shape[1]
    seqs = 4 * nzh
    piece = keys_per // (2 * ny)

    qkv_rows = rows_here + 2 * kv_rows

    def shard_at(hop, at_zl, at_x):
        return (lax.rem(zh + (nzh - hop), nzh) * 2 + at_zl) * 2 + at_x

    packed = pack(zl, w_query, w_keyval, w_out, hidden, cotangent)
    other_qkv, other_out, own, own_q, own_kv, own_out, states = packed
    up2, down2 = flip(enc_up, "c"), flip(enc_down, "c")
    beside_qkv = flip(other_qkv, "zl")
    own_x = flip(own, "x")
    hop_q = onward(own_q, "zh")

    def gather_states(rows):
        return lax.all_gather(rows, ("y", "c"), axis=0, tiled=False)

    own_states = gather_states(states)

    ids = neighbour_ids.reshape(spans_here, 2, ny, piece).transpose(1, 2, 0, 3).reshape(-1)
    vocab_here = embed_table.shape[0]
    local_ids = tie(ids, other_qkv) - (y * 2 + c) * vocab_here
    inside = jnp.logical_and(local_ids >= 0, local_ids < vocab_here)
    clipped = jnp.clip(local_ids, 0, vocab_here - 1)
    picked = tie(embed_table.at[clipped].get(mode="promise_in_bounds"), hop_q, beside_qkv, up2, down2)
    half_rows = ids.shape[0] // 2

    def half_emb(core):
        rows = lax.dynamic_slice_in_dim(picked, core * half_rows, half_rows, 0)
        live = lax.dynamic_slice_in_dim(inside, core * half_rows, half_rows, 0)
        return jnp.where(live[:, None], rows, jnp.zeros((), BF16))

    emb_other = half_emb(1 - c)
    emb = tie(half_emb(c), own_x) + flip(emb_other, "c")

    beside_qkv, other_out, hop_q = (tie(a, emb) for a in (beside_qkv, other_out, hop_q))
    beside_qkv_x, hop_q_x = flip(beside_qkv, "x"), flip(hop_q, "x")
    hop_q2 = onward(beside_qkv[:rows_here], "zh")
    beside_out = flip(other_out, "zl")
    emb = emb + flip(emb, "y") if ny == 2 else lax.psum(emb, "y")
    emb = tie(emb, beside_qkv_x, hop_q_x, hop_q2, beside_out, own_states)

    own_kv, beside_out, states = (tie(a, emb) for a in (own_kv, beside_out, states))
    hop_kv = onward(own_kv, "zh")
    beside_out_x = flip(beside_out, "x")
    other_states = flip(states, "zl")
    share_rows = half_rows // ny
    ffn, share = encode(y, emb, [enc_up, enc_down, up2, down2], share_rows, 2)
    ffn = tie(ffn, hop_kv)
    hop_kv2 = onward(tie(beside_qkv, ffn)[rows_here:], "zh")
    if ny == 2:
        sent = lax.dynamic_slice_in_dim(ffn, (1 - y) * share_rows, share_rows, 0)
        share = share + flip(sent, "y").astype(F32)
    else:
        share = lax.psum_scatter(ffn, "y", scatter_dimension=0, tiled=True).astype(F32)
        share = share + lax.dynamic_slice_in_dim(emb, y * share_rows, share_rows, 0).astype(F32)
    encoded = rms_rows(tie(share, beside_out_x, other_states, hop_kv2)).astype(BF16)

    other_states = gather_states(tie(other_states, encoded))
    before = lax.ppermute(encoded[share_rows - piece :], SEQ, [(i, i + 1) for i in range(seqs - 1)])
    encoded = jnp.concatenate([before, encoded], axis=0)
    hop_qkv = jnp.concatenate([tie(hop_q2, encoded), hop_kv, hop_kv2], axis=0)
    hop_qkv_x = flip(hop_qkv, "x")
    hop_out = onward(jnp.concatenate([tie(own_out, encoded), beside_out], axis=0), "zh")

    if ny == 2:
        corner = lax.ppermute(encoded, ("zl", "y"), [(i, 3 - i) for i in range(4)])
        over_y, over_zl = flip(encoded, "y"), flip(encoded, "zl")
        over_y = tie(over_y, hop_qkv_x)
        own_rows, other_rows = [encoded, over_y], [over_zl, corner]
        ys = [y, 1 - y]
    else:
        own_rows = [lax.all_gather(encoded, "y", axis=0, tiled=True)]
        other_rows, over_y = [flip(own_rows[0], "zl")], own_rows[0]
        ys = [jnp.int32(i) for i in range(ny)]

    q_pieces, kv_pieces, out_pieces = [], [], []

    def add_kv(at, block, start):
        kv_pieces.append((at, block, start, kv_rows, 0))
        kv_pieces.append((at, block, start + kv_rows, kv_rows, 1))

    here, here_x = shard_at(0, zl, x), shard_at(0, zl, 1 - x)
    there, there_x = shard_at(0, 1 - zl, x), shard_at(0, 1 - zl, 1 - x)
    for at, block, start in ((here, own_q, 0), (here_x, own_x, 0), (there, beside_qkv, 0), (there_x, beside_qkv_x, 0)):
        q_pieces.append((at, block, start, rows_here, None))
    for at, block, start in (
        (here, own_kv, 0),
        (here_x, own_x, rows_here),
        (there, beside_qkv, rows_here),
        (there_x, beside_qkv_x, rows_here),
    ):
        add_kv(at, block, start)
    for at, block, start in ((here, own_out, 0), (here_x, own_x, qkv_rows), (there, beside_out, 0), (there_x, beside_out_x, 0)):
        out_pieces.append((at, block, start, rows_here, None))
    for hop in range(1, nzh):
        if hop > 1:
            hop_q, hop_qkv = onward(hop_q, "zh"), onward(hop_qkv, "zh")
            hop_q_x, hop_qkv_x = flip(hop_q, "x"), flip(hop_qkv, "x")
        for at_x, at_q, at_qkv in ((x, hop_q, hop_qkv), (1 - x, hop_q_x, hop_qkv_x)):
            here, there = shard_at(hop, zl, at_x), shard_at(hop, 1 - zl, at_x)
            q_pieces += [(here, at_q, 0, rows_here, None), (there, at_qkv, 0, rows_here, None)]
            add_kv(here, at_qkv, rows_here)
            add_kv(there, at_qkv, qkv_rows)

    lens_pad = jnp.concatenate([jnp.ones((1, neigh), jnp.int32), neighbour_lengths], axis=0)
    at = []
    for turn in range(2):
        first = ((zh * 2 + lax.rem(zl + turn, 2)) * 2 + x) * spans_here
        rows = lax.dynamic_slice_in_dim(lens_pad, first, groups, 0)
        live = (first + jnp.arange(groups, dtype=jnp.int32) > 0).astype(jnp.int32)
        at.append(jnp.concatenate([rows, live[:, None]], axis=1).reshape(-1))
    starts = [(core * ny + at_y) * piece for core in (c, 1 - c) for at_y in ys]
    at = jnp.concatenate(at + [jnp.stack(starts).astype(jnp.int32)])

    w_dims = (seqs * rows_here, inner)
    q_pieces[0] = (q_pieces[0][0], tie(q_pieces[0][1], over_y)) + q_pieces[0][2:]
    kv_pieces[0] = (kv_pieces[0][0], tie(kv_pieces[0][1], over_y)) + kv_pieces[0][2:]
    wkv = place(kv_pieces, (2, enc_width, inner))
    wq, wo = place(q_pieces, w_dims), place(out_pieces, w_dims)
    every = jnp.arange(2 * ny, dtype=jnp.int32)
    kv_shape = (ny, groups, piece, inner)
    states = (own_states, other_states)

    def at_of(pieces):
        return jnp.stack([p[0] for p in pieces])

    def keys_values(rows, rows2):
        near = keyval(at, rows, wkv)
        far = keyval(at, tie(rows2, *near), wkv)
        return [a.reshape(kv_shape) for a in (*near, *far)]

    def attend(turn, kv, query):
        return over_shard(attend_kernel, turn, at, query, kv, span, head_dim, None)

    own_rows = jnp.concatenate(own_rows, axis=0)
    own_rows2 = flip(own_rows, "c")
    kv = keys_values(own_rows, own_rows2)
    query = project(every, states, 0, tie(wq, wo, *kv), hidden.shape[1], span, True)
    attn, prob = attend(0, kv, query)
    other_rows = jnp.concatenate(lax.optimization_barrier((*other_rows, attn))[:-1], axis=0)
    other_rows2 = flip(other_rows, "c")
    hop_out = tie(hop_out, attn)
    hop_out_x = flip(hop_out, "x")
    kv2 = keys_values(other_rows, other_rows2)
    attn2, prob2 = attend(1, kv2, query)
    some = project(at_of(out_pieces), states, 1, tie(wo, attn2), rows_here, span, False)

    late = []
    for hop in range(1, nzh):
        if hop > 1:
            hop_out = onward(hop_out, "zh")
            hop_out_x = flip(hop_out, "x")
        for at_x, block in ((x, hop_out), (1 - x, hop_out_x)):
            late.append((shard_at(hop, zl, at_x), block, 0, rows_here, None))
            late.append((shard_at(hop, 1 - zl, at_x), block, rows_here, rows_here, None))

    hop_out_x = tie(hop_out_x, some)
    late[-2:] = [(p[0], hop_out_x) + p[2:] for p in late[-2:]]
    wo = place(late, w_dims, wo)
    attn = (attn, attn2)
    out_sent = core_sums(attn, wo)
    if out_sent is not None:
        some = tie(some, out_sent)
    d_attn = project(at_of(late), states, 1, wo, rows_here, span, True, some)
    cca_out, moved, arrived = sum_heads((attn[0], tie(attn[1], d_attn)), wo, out_sent)
    d_attn = tie(d_attn, *moved)
    d_query = [
        over_shard(backward_kernel, turn, at, d_attn, kv_here, span, head_dim, prob_here)[0]
        for turn, kv_here, prob_here in ((0, kv, prob), (1, kv2, prob2))
    ]
    grad_sent = core_sums(d_query, wq)
    if arrived:
        grad_sent = tie(grad_sent, *arrived[1:])
    hidden_grad, _, _ = sum_heads(d_query, wq, grad_sent)
    return (cca_out, hidden_grad)


def solution(mesh):
    ns, nm = mesh.shape["seq"], mesh.shape["mp"]
    fine = Mesh(mesh.devices.reshape(ns // 4, 2, 2, nm // 2, 2), ("zh", "zl", "x", "y", "c"))
    seq, mp = SEQ, ("y", "c")
    return jax.shard_map(
        per_device,
        mesh=fine,
        in_specs=(
            P(seq, mp),
            P(seq, mp),
            P(seq, None, None),
            P(),
            P(mp, None),
            P(mp, None),
            P(mp, None),
            P(seq, mp, None),
            P(seq, mp, None, None),
            P(seq, mp, None),
        ),
        out_specs=(P(seq, mp), P(seq, mp)),
        check_vma=False,
    )
```

```python
import functools

import jax
import jax.numpy as jnp
from jax import lax
from jax.experimental import pallas as pl
from jax.experimental.pallas import tpu as pltpu
from jax.sharding import Mesh
from jax.sharding import PartitionSpec as P

SEQ = ("zh", "zl", "x")
GROUP = ("zl", "y", "c")
VMEM = 62 * 1024 * 1024
F32 = jnp.float32
BF16 = jnp.bfloat16


def flip(shard, axis):
    return lax.ppermute(shard, axis, [(0, 1), (1, 0)])


def onward(shard, axis):
    count = lax.axis_size(axis)
    return lax.ppermute(shard, axis, [(i, (i + 1) % count) for i in range(count)])


def tie(value, *earlier):
    return lax.optimization_barrier((value,) + earlier)[0]


def rms_rows(values):
    return values * lax.rsqrt(jnp.mean(values * values, axis=-1, keepdims=True) + 1e-06)


def dot(left, right):
    return jnp.dot(left, right, preferred_element_type=F32)


def dot_t(left, right):
    return lax.dot_general(left, right, (((1,), (1,)), ((), ())), preferred_element_type=F32)


def call(kernel, grid, prefetch, operands, outs, scratch):
    arrays = [o[0] for o in operands]
    return pl.pallas_call(
        kernel,
        grid_spec=pltpu.PrefetchScalarGridSpec(
            num_scalar_prefetch=1,
            grid=grid,
            in_specs=[pl.BlockSpec(block, index) for _, block, index in operands],
            out_specs=[pl.BlockSpec(block, index) for _, block, index in outs],
            scratch_shapes=scratch,
        ),
        out_shape=[o[0] for o in outs],
        compiler_params=pltpu.CompilerParams(vmem_limit_bytes=VMEM),
        cost_estimate=pl.CostEstimate(flops=20000000000, bytes_accessed=1, transcendentals=0),
    )(prefetch, *arrays)


def shape(dims, dtype):
    return jax.ShapeDtypeStruct(dims, dtype)


def whole_block(ndim):
    return lambda *_: (0,) * ndim


def pack_kernel(
    at_ref, q_ref, kv_ref, o_ref, h_ref, c_ref,
    other_qkv_ref, other_out_ref, own_ref, own_q_ref, own_kv_ref, own_out_ref, states_ref,
    q, kv, o,
):
    rows, inner = own_out_ref.shape
    kv_rows, heads, _, head_dim = kv_ref.shape
    q[...] = q_ref[...].reshape(q.shape)
    o[...] = o_ref[...].reshape(o.shape)
    kv[...] = kv_ref[...].reshape(kv.shape)

    def cut(of, start, size):
        return of[:, pl.ds(pl.multiple_of(start, head_dim), size)]

    def copy(which, q_dst, kv_dst, out_dst):
        q_dst[...] = cut(q, which * inner, inner)
        out_dst[...] = cut(o, which * inner, inner)
        for h in range(heads // 2):
            for i in range(2):
                piece = cut(kv, ((which * (heads // 2) + h) * 2 + i) * head_dim, head_dim)
                kv_dst[i * kv_rows : (i + 1) * kv_rows, h * head_dim : (h + 1) * head_dim] = piece

    zl = at_ref[0]
    kv_end = rows + 2 * kv_rows
    copy(1 - zl, other_qkv_ref.at[:rows], other_qkv_ref.at[rows:], other_out_ref)
    copy(zl, own_ref.at[:rows], own_ref.at[rows:kv_end], own_ref.at[kv_end:])
    copy(zl, own_q_ref, own_kv_ref, own_out_ref)
    states_ref[0] = h_ref[...]
    states_ref[1] = c_ref[...]


def pack(zl, w_query, w_keyval, w_out, hidden, cotangent):
    rows, heads, head_dim = w_query.shape
    kv_rows, inner = w_keyval.shape[0], heads // 2 * head_dim
    sizes = [rows + 2 * kv_rows, rows, 2 * rows + 2 * kv_rows, rows, 2 * kv_rows, rows]
    outs = [(n, inner) for n in sizes] + [(2,) + hidden.shape]
    return call(
        pack_kernel,
        (1,),
        zl.reshape(1),
        [(a, a.shape, whole_block(a.ndim)) for a in (w_query, w_keyval, w_out, hidden, cotangent)],
        [(shape(dims, BF16), dims, whole_block(len(dims))) for dims in outs],
        [pltpu.VMEM(dims, BF16) for dims in ((rows, 2 * inner), (kv_rows, 4 * inner), (rows, 2 * inner))],
    )


def place_kernel(jobs, count, through, at_ref, *refs):
    sources, out_ref, sems = refs[:count], refs[count + through], refs[-1]
    stage = refs[-2] if through else out_ref

    def dst(ref, i, rows, plane):
        to = pl.ds(pl.multiple_of(at_ref[i] * rows, 16), rows)
        return ref.at[to] if plane is None else ref.at[plane, to]

    copies = []
    for i, (source, start, rows, plane) in enumerate(jobs):
        src = sources[source].at[pl.ds(start, rows)]
        to = stage.at[pl.ds(i * rows, rows)] if through else dst(stage, i, rows, plane)
        copies.append(pltpu.make_async_copy(src, to, sems.at[i]))
    for copy in copies:
        copy.start()
    for copy in copies:
        copy.wait()
    if through:
        copies = []
        for i, (_, _, rows, plane) in enumerate(jobs):
            src = stage.at[pl.ds(i * rows, rows)]
            copies.append(pltpu.make_async_copy(src, dst(out_ref, i, rows, plane), sems.at[i]))
        for copy in copies:
            copy.start()
        for copy in copies:
            copy.wait()


def place(pieces, dims, base=None):
    sources = []
    for piece in pieces:
        if not any(piece[1] is a for a in sources):
            sources.append(piece[1])
    index = [next(i for i, a in enumerate(sources) if a is piece[1]) for piece in pieces]
    jobs = [(i, p[2], p[3], p[4]) for i, p in zip(index, pieces)]
    if any(rows % 16 for _, _, rows, _ in jobs):
        whole = jnp.zeros(dims, BF16) if base is None else base
        for (at, block, start, rows, plane) in pieces:
            block = block[start : start + rows]
            if plane is None:
                whole = lax.dynamic_update_slice(whole, block, (at * rows, 0))
            else:
                whole = lax.dynamic_update_slice(whole, block[None], (plane, at * rows, 0))
        return whole
    through = base is not None
    arrays = sources + [base] if through else sources
    scratch = [pltpu.SemaphoreType.DMA((len(jobs),))]
    if through:
        scratch.insert(0, pltpu.VMEM((len(jobs) * jobs[0][2], dims[-1]), BF16))
    out_spec = pl.BlockSpec(memory_space=pl.ANY) if through else pl.BlockSpec(dims, whole_block(len(dims)))
    return pl.pallas_call(
        functools.partial(place_kernel, jobs, len(sources), int(through)),
        grid_spec=pltpu.PrefetchScalarGridSpec(
            num_scalar_prefetch=1,
            grid=(1,),
            in_specs=[pl.BlockSpec(memory_space=pl.ANY)] * len(arrays),
            out_specs=out_spec,
            scratch_shapes=scratch,
        ),
        out_shape=shape(dims, BF16),
        input_output_aliases={len(arrays): 0} if through else {},
        compiler_params=pltpu.CompilerParams(vmem_limit_bytes=VMEM),
        cost_estimate=pl.CostEstimate(flops=20000000000, bytes_accessed=1, transcendentals=0),
    )(jnp.stack([p[0] for p in pieces]).astype(jnp.int32), *arrays)


def project_kernel(span, first, last, at_ref, own_ref, other_ref, w_ref, *rest):
    out_ref, acc = rest[-2:]
    step = pl.program_id(0)
    toks, cols = own_ref.shape[0], acc.shape[1]
    rows = jnp.concatenate([own_ref[...], other_ref[...]], axis=0)
    part = dot(rows, w_ref[...])

    @pl.when(step == 0)
    def _():
        acc[...] = part if first else part + rest[0][...]

    @pl.when(step > 0)
    def _():
        acc[...] += part

    @pl.when(step == pl.num_programs(0) - 1)
    def _():
        if not last:
            out_ref[...] = acc[...]
            return
        front, back = jnp.zeros((1, cols), F32), jnp.zeros((span - 1, cols), F32)
        for s in range(2):
            own = acc[s * toks : (s + 1) * toks, :]
            out_ref[s] = jnp.concatenate([front, own, back], axis=0).astype(BF16)


def project(at, states, which, w, wide, span, last, before=None):
    toks, wm = states[0].shape[2:]
    cols, steps, per = w.shape[1], at.shape[0], wm // wide
    operands = [
        (a, (None, None, toks, wide), lambda i, at: (at[i] // per, which, 0, lax.rem(at[i], per)))
        for a in states
    ]
    operands += [
        (w, (wide, cols), lambda i, at: (at[i], 0)),
    ]
    total = (2 * toks, cols)
    if before is not None:
        operands.append((before, total, whole_block(2)))
    out = shape((2, toks + span, cols), BF16) if last else shape(total, F32)
    return call(
        functools.partial(project_kernel, span, before is None, last),
        (steps,),
        at,
        operands,
        [(out, out.shape, whole_block(len(out.shape)))],
        [pltpu.VMEM(total, F32)],
    )[0]


def keyval_kernel(at_ref, rows_ref, w_ref, k_ref, v_ref):
    rows = rows_ref[...]
    k_ref[...] = dot(rows, w_ref[0]).astype(BF16)
    v_ref[...] = dot(rows, w_ref[1]).astype(BF16)


def keyval(at, rows, w):
    out = shape((rows.shape[0], w.shape[2]), BF16)
    operands = [(a, a.shape, whole_block(a.ndim)) for a in (rows, w)]
    return call(keyval_kernel, (1,), at, operands, [(out, out.shape, whole_block(2))] * 2, [])


def encode_kernel(at_ref, emb_ref, up_ref, down_ref, up2_ref, down2_ref, ffn_ref, own_ref, normed, acc):
    step = pl.program_id(0)

    @pl.when(step == 0)
    def _():
        normed[...] = rms_rows(emb_ref[...].astype(F32)).astype(BF16)

    part = 0.0
    for up, down in ((up_ref, down_ref), (up2_ref, down2_ref)):
        act = jax.nn.gelu(dot_t(normed[...], up[...])).astype(BF16)
        part = part + dot(act, down[...])

    @pl.when(step == 0)
    def _():
        acc[...] = part

    @pl.when(step > 0)
    def _():
        acc[...] += part

    @pl.when(step == pl.num_programs(0) - 1)
    def _():
        share = own_ref.shape[0]
        ffn_ref[...] = acc[...].astype(BF16)
        mine = pl.ds(pl.multiple_of(at_ref[0] * share, share), share)
        own_ref[...] = acc[mine, :] + emb_ref[mine, :].astype(F32)


def encode(y, emb, weights, share, tiles):
    count, width = emb.shape
    hidden = weights[0].shape[0]
    tile = hidden // tiles
    return call(
        encode_kernel,
        (tiles,),
        y.reshape(1),
        [(emb, emb.shape, whole_block(2))]
        + [(w, (tile, width), lambda i, at: (i, 0)) for w in weights],
        [
            (shape((count, width), BF16), (count, width), whole_block(2)),
            (shape((share, width), F32), (share, width), whole_block(2)),
        ],
        [pltpu.VMEM((count, width), BF16), pltpu.VMEM((count, width), F32)],
    )


def span_rows(halves, g, cols):
    parts = [half[:, g, :, cols] for half in halves]
    parts = [p.reshape(p.shape[0] * p.shape[1], p.shape[2]) for p in parts]
    return jnp.concatenate(parts, axis=0)


def attend_kernel(span, head_dim, turn, at_ref, q_ref, k_ref, v_ref, k2_ref, v2_ref, attn_ref, prob_ref, stage):
    blocks, groups, piece, inner = k_ref.shape
    heads, keys_per = inner // head_dim, 2 * blocks * piece
    nlen = keys_per // 2
    scale = head_dim ** (-0.5)
    toks = attn_ref.shape[0]
    lane = lax.broadcasted_iota(jnp.int32, (span, keys_per), 1)
    key = lane
    for i in range(2 * blocks):
        start = at_ref[2 * groups * 3 + i]
        here = jnp.logical_and(lane >= i * piece, lane < (i + 1) * piece)
        key = jnp.where(here, lane + (start - i * piece), key)
    for g in range(groups):
        rows = pl.ds(g * span, span)
        for h in range(heads):
            cols = pl.ds(h * head_dim, head_dim)
            prob_ref[h, rows, :] = dot_t(q_ref[0, rows, cols], span_rows((k_ref, k2_ref), g, cols))
    for g in range(groups):
        rows = pl.ds(g * span, span)
        base = (turn * groups + g) * 3
        first, second, live = at_ref[base], at_ref[base + 1], at_ref[base + 2]
        mask = jnp.logical_or(key < first, jnp.logical_and(key >= nlen, key < nlen + second))
        weight = live.astype(F32)
        for h in range(heads):
            cols = pl.ds(h * head_dim, head_dim)
            expo = jnp.where(mask, jnp.exp(prob_ref[h, rows, :] * scale), 0.0)
            prob = expo * (weight / jnp.sum(expo, axis=-1, keepdims=True))
            prob_ref[h, rows, :] = prob
            stage[rows, cols] = dot(prob.astype(BF16), span_rows((v_ref, v2_ref), g, cols))
    attn_ref[...] = stage[1 : toks + 1, :].astype(BF16)


def backward_kernel(span, head_dim, at_ref, *refs):
    (d_ref, w_ref, w2_ref), shards, (dq_ref, dq2_ref, sent_ref, stage, d_prob) = refs[:3], refs[3:-5], refs[-5:]
    for turn, out_ref in enumerate((dq_ref, dq2_ref)):
        prob_ref, k_ref, v_ref, k2_ref, v2_ref = shards[5 * turn : 5 * turn + 5]
        groups, inner = k_ref.shape[1], k_ref.shape[3]
        heads = inner // head_dim
        scale = head_dim ** (-0.5)
        for g in range(groups):
            rows = pl.ds(g * span, span)
            for h in range(heads):
                cols = pl.ds(h * head_dim, head_dim)
                d_prob[turn, h, rows, :] = dot_t(d_ref[turn, rows, cols], span_rows((v_ref, v2_ref), g, cols))
        for g in range(groups):
            rows = pl.ds(g * span, span)
            for h in range(heads):
                cols = pl.ds(h * head_dim, head_dim)
                prob, slope = prob_ref[h, rows, :], d_prob[turn, h, rows, :]
                delta = jnp.sum(prob * slope, axis=-1, keepdims=True)
                d_score = (prob * (slope - delta) * scale).astype(BF16)
                stage[turn, rows, cols] = dot(d_score, span_rows((k_ref, k2_ref), g, cols))
        out_ref[...] = stage[turn, 1 : out_ref.shape[0] + 1, :].astype(BF16)
    rows = jnp.concatenate([dq_ref[...], dq2_ref[...]], axis=0)
    sent_ref[0] = dot_t(rows, w_ref[...]).astype(BF16)
    sent_ref[1] = dot_t(rows, w2_ref[...]).astype(BF16)


def backward(probs, d_attn, kvs, w, span, head_dim):
    y, c = lax.axis_index("y"), lax.axis_index("c")
    wm = w.shape[0] // (2 * lax.axis_size("y"))
    at = jnp.stack([(1 - y) * 2 + (1 - c), y * 2 + (1 - c)])
    shards, rows, inner = d_attn.shape
    toks = rows - span
    operands = [(d_attn, d_attn.shape, whole_block(3))]
    operands += [(w, (wm, inner), lambda i, at, j=j: (at[j], 0)) for j in range(2)]
    for prob, kv in zip(probs, kvs):
        operands += [(a, a.shape, whole_block(a.ndim)) for a in (prob, *kv)]
    dims = [(toks, inner), (toks, inner), (2, 2 * toks, wm)]
    return call(
        functools.partial(backward_kernel, span, head_dim),
        (1,),
        at,
        operands,
        [(shape(d, BF16), d, whole_block(len(d))) for d in dims],
        [pltpu.VMEM(d_attn.shape, F32), pltpu.VMEM((shards,) + probs[0].shape, F32)],
    )


def attend(turn, at, padded, kv, span, head_dim):
    _, rows, inner = padded.shape
    toks, heads = rows - span, inner // head_dim
    probs = shape((heads, rows, 2 * kv[0].shape[0] * kv[0].shape[2]), F32)
    operands = [(padded, (1, rows, inner), lambda i, at: (turn, 0, 0))]
    operands += [(a, a.shape, whole_block(4)) for a in kv]
    outs = [(shape((toks, inner), BF16), (toks, inner), whole_block(2)), (probs, probs.shape, whole_block(3))]
    scratch = [pltpu.VMEM((rows, inner), F32)]
    return call(functools.partial(attend_kernel, span, head_dim, turn), (1,), at, operands, outs, scratch)


def sent_kernel(at_ref, own_ref, other_ref, w_ref, out_ref):
    rows = jnp.concatenate([own_ref[...], other_ref[...]], axis=0)
    out_ref[0] = dot_t(rows, w_ref[...]).astype(BF16)


def kept_kernel(at_ref, own_rows_ref, other_rows_ref, w_ref, add_ref, both_ref, y_ref, zl_ref, own_ref):
    def total(rows_ref, start):
        add = add_ref[0, start : start + rows_ref.shape[0], :]
        return dot_t(rows_ref[...], w_ref[...]) + add.astype(F32)

    @pl.when(pl.program_id(0) == 0)
    def _():
        y_ref[...] = total(own_rows_ref, 0).astype(BF16)
        both_ref[...] = total(other_rows_ref, own_ref.shape[0]).astype(BF16)

    @pl.when(pl.program_id(0) == 1)
    def _():
        own_ref[...] = total(own_rows_ref, 0)
        zl_ref[...] = total(other_rows_ref, own_ref.shape[0]).astype(BF16)


def columns(at, rows, w, wm, add=None):
    toks, inner = rows[0].shape
    operands = [(a, a.shape, whole_block(2)) for a in rows]
    operands.append((w, (wm, inner), lambda i, at: (at[i], 0)))
    moved = (1, 2 * toks, wm), lambda i, at: (i, 0, 0)
    if add is None:
        out = shape((2, 2 * toks, wm), BF16)
        return call(sent_kernel, (2,), at, operands, [(out,) + moved], [])[0]
    operands.append((add,) + moved)
    outs = [(shape((toks, wm), dtype), (toks, wm), whole_block(2)) for dtype in (BF16, BF16, BF16, F32)]
    return call(kept_kernel, (2,), at, operands, outs, [])


def core_sums(rows, w):
    y, c = lax.axis_index("y"), lax.axis_index("c")
    ny = lax.axis_size("y")
    wm = w.shape[0] // (2 * ny)
    if ny != 2:
        return None
    return columns(jnp.stack([(1 - y) * 2 + (1 - c), y * 2 + (1 - c)]), rows, w, wm)


def sum_heads(rows, w, sent):
    zl, y, c = (lax.axis_index(name) for name in GROUP)
    ny = lax.axis_size("y")
    wm = w.shape[0] // (2 * ny)
    if ny != 2:
        rows = jnp.concatenate(rows, axis=0)
        count = rows.shape[0]
        rows = jnp.roll(rows, zl * (count // 2), axis=0)
        blocks = dot_t(rows, w).astype(BF16).reshape(2, count // 2, ny, 2, wm)
        blocks = blocks.transpose(0, 2, 3, 1, 4).reshape(ny * 2 * count, wm)
        return lax.psum_scatter(blocks, GROUP, scatter_dimension=0, tiled=True).astype(BF16), (), ()
    at = jnp.stack([(1 - y) * 2 + c, y * 2 + c])
    to_both, to_y, to_zl, own = columns(at, rows, w, wm, flip(sent, "c"))
    over_both = lax.ppermute(to_both, ("zl", "y"), [(i, 3 - i) for i in range(4)])
    over_y, over_zl = flip(to_y, "y"), flip(to_zl, "zl")
    total = own + over_zl.astype(F32) + over_y.astype(F32) + over_both.astype(F32)
    return total.astype(BF16), (to_both, to_y, to_zl), (over_both, over_y, over_zl)


def per_device(
    hidden,
    cotangent,
    neighbour_ids,
    neighbour_lengths,
    embed_table,
    enc_up,
    enc_down,
    w_query,
    w_keyval,
    w_out,
):
    zh, zl, x = (lax.axis_index(name) for name in SEQ)
    y, c = lax.axis_index("y"), lax.axis_index("c")
    nzh, ny = lax.axis_size("zh"), lax.axis_size("y")
    spans_here, neigh, nlen = neighbour_ids.shape
    toks = hidden.shape[0]
    span = toks // spans_here
    keys_per = neigh * nlen
    groups = spans_here + 1
    rows_here, heads_here, head_dim = w_query.shape
    heads = heads_here // 2
    inner = heads * head_dim
    kv_rows, enc_width = w_keyval.shape[0], embed_table.shape[1]
    seqs = 4 * nzh
    piece = keys_per // (2 * ny)

    qkv_rows = rows_here + 2 * kv_rows

    def shard_at(hop, at_zl, at_x):
        return (lax.rem(zh + (nzh - hop), nzh) * 2 + at_zl) * 2 + at_x

    packed = pack(zl, w_query, w_keyval, w_out, hidden, cotangent)
    other_qkv, other_out, own, own_q, own_kv, own_out, states = packed
    up2, down2 = flip(enc_up, "c"), flip(enc_down, "c")
    beside_qkv = flip(other_qkv, "zl")
    own_x = flip(own, "x")
    hop_q = onward(own_q, "zh")

    def gather_states(rows):
        return lax.all_gather(rows, ("y", "c"), axis=0, tiled=False)

    own_states = gather_states(states)

    ids = neighbour_ids.reshape(spans_here, 2, ny, piece).transpose(1, 2, 0, 3).reshape(-1)
    vocab_here = embed_table.shape[0]
    local_ids = tie(ids, other_qkv) - (y * 2 + c) * vocab_here
    inside = jnp.logical_and(local_ids >= 0, local_ids < vocab_here)
    clipped = jnp.clip(local_ids, 0, vocab_here - 1)
    picked = tie(embed_table.at[clipped].get(mode="promise_in_bounds"), hop_q, beside_qkv, up2, down2)
    half_rows = ids.shape[0] // 2

    def half_emb(core):
        rows = lax.dynamic_slice_in_dim(picked, core * half_rows, half_rows, 0)
        live = lax.dynamic_slice_in_dim(inside, core * half_rows, half_rows, 0)
        return jnp.where(live[:, None], rows, jnp.zeros((), BF16))

    emb_other = half_emb(1 - c)
    emb = tie(half_emb(c), own_x) + flip(emb_other, "c")

    beside_qkv, other_out, hop_q = (tie(a, emb) for a in (beside_qkv, other_out, hop_q))
    beside_qkv_x, hop_q_x = flip(beside_qkv, "x"), flip(hop_q, "x")
    hop_q2 = onward(beside_qkv[:rows_here], "zh")
    beside_out = flip(other_out, "zl")
    emb = emb + flip(emb, "y") if ny == 2 else lax.psum(emb, "y")
    emb = tie(emb, beside_qkv_x, hop_q_x, hop_q2, beside_out, own_states)

    own_kv, beside_out, states = (tie(a, emb) for a in (own_kv, beside_out, states))
    hop_kv = onward(own_kv, "zh")
    beside_out_x = flip(beside_out, "x")
    other_states = flip(states, "zl")
    share_rows = half_rows // ny
    ffn, share = encode(y, emb, [enc_up, enc_down, up2, down2], share_rows, 2)
    ffn = tie(ffn, hop_kv)
    hop_kv2 = onward(tie(beside_qkv, ffn)[rows_here:], "zh")
    if ny == 2:
        sent = lax.dynamic_slice_in_dim(ffn, (1 - y) * share_rows, share_rows, 0)
        share = share + flip(sent, "y").astype(F32)
    else:
        share = lax.psum_scatter(ffn, "y", scatter_dimension=0, tiled=True).astype(F32)
        share = share + lax.dynamic_slice_in_dim(emb, y * share_rows, share_rows, 0).astype(F32)
    encoded = rms_rows(tie(share, beside_out_x, other_states, hop_kv2)).astype(BF16)

    other_states = gather_states(tie(other_states, encoded))
    before = lax.ppermute(encoded[share_rows - piece :], SEQ, [(i, i + 1) for i in range(seqs - 1)])
    encoded = jnp.concatenate([before, encoded], axis=0)
    hop_qkv = jnp.concatenate([tie(hop_q2, encoded), hop_kv, hop_kv2], axis=0)
    hop_qkv_x = flip(hop_qkv, "x")
    hop_out = onward(jnp.concatenate([tie(own_out, encoded), beside_out], axis=0), "zh")

    if ny == 2:
        corner = lax.ppermute(encoded, ("zl", "y"), [(i, 3 - i) for i in range(4)])
        over_y, over_zl = flip(encoded, "y"), flip(encoded, "zl")
        over_y = tie(over_y, hop_qkv_x)
        own_rows, other_rows = [encoded, over_y], [over_zl, corner]
        ys = [y, 1 - y]
    else:
        own_rows = [lax.all_gather(encoded, "y", axis=0, tiled=True)]
        other_rows, over_y = [flip(own_rows[0], "zl")], own_rows[0]
        ys = [jnp.int32(i) for i in range(ny)]

    q_pieces, kv_pieces, out_pieces = [], [], []

    def add_kv(at, block, start):
        kv_pieces.append((at, block, start, kv_rows, 0))
        kv_pieces.append((at, block, start + kv_rows, kv_rows, 1))

    here, here_x = shard_at(0, zl, x), shard_at(0, zl, 1 - x)
    there, there_x = shard_at(0, 1 - zl, x), shard_at(0, 1 - zl, 1 - x)
    for at, block, start in ((here, own_q, 0), (here_x, own_x, 0), (there, beside_qkv, 0), (there_x, beside_qkv_x, 0)):
        q_pieces.append((at, block, start, rows_here, None))
    for at, block, start in (
        (here, own_kv, 0),
        (here_x, own_x, rows_here),
        (there, beside_qkv, rows_here),
        (there_x, beside_qkv_x, rows_here),
    ):
        add_kv(at, block, start)
    for at, block, start in ((here, own_out, 0), (here_x, own_x, qkv_rows), (there, beside_out, 0), (there_x, beside_out_x, 0)):
        out_pieces.append((at, block, start, rows_here, None))
    for hop in range(1, nzh):
        if hop > 1:
            hop_q, hop_qkv = onward(hop_q, "zh"), onward(hop_qkv, "zh")
            hop_q_x, hop_qkv_x = flip(hop_q, "x"), flip(hop_qkv, "x")
        for at_x, at_q, at_qkv in ((x, hop_q, hop_qkv), (1 - x, hop_q_x, hop_qkv_x)):
            here, there = shard_at(hop, zl, at_x), shard_at(hop, 1 - zl, at_x)
            q_pieces += [(here, at_q, 0, rows_here, None), (there, at_qkv, 0, rows_here, None)]
            add_kv(here, at_qkv, rows_here)
            add_kv(there, at_qkv, qkv_rows)

    lens_pad = jnp.concatenate([jnp.ones((1, neigh), jnp.int32), neighbour_lengths], axis=0)
    at = []
    for turn in range(2):
        first = ((zh * 2 + lax.rem(zl + turn, 2)) * 2 + x) * spans_here
        rows = lax.dynamic_slice_in_dim(lens_pad, first, groups, 0)
        live = (first + jnp.arange(groups, dtype=jnp.int32) > 0).astype(jnp.int32)
        at.append(jnp.concatenate([rows, live[:, None]], axis=1).reshape(-1))
    starts = [(core * ny + at_y) * piece for core in (c, 1 - c) for at_y in ys]
    at = jnp.concatenate(at + [jnp.stack(starts).astype(jnp.int32)])

    w_dims = (seqs * rows_here, inner)
    q_pieces[0] = (q_pieces[0][0], tie(q_pieces[0][1], over_y)) + q_pieces[0][2:]
    kv_pieces[0] = (kv_pieces[0][0], tie(kv_pieces[0][1], over_y)) + kv_pieces[0][2:]
    wkv = place(kv_pieces, (2, enc_width, inner))
    wq, wo = place(q_pieces, w_dims), place(out_pieces, w_dims)
    every = jnp.arange(2 * ny, dtype=jnp.int32)
    kv_shape = (ny, groups, piece, inner)
    states = (own_states, other_states)

    def at_of(pieces):
        return jnp.stack([p[0] for p in pieces])

    def keys_values(rows, rows2):
        near = keyval(at, rows, wkv)
        far = keyval(at, tie(rows2, *near), wkv)
        return [a.reshape(kv_shape) for a in (*near, *far)]

    own_rows = jnp.concatenate(own_rows, axis=0)
    own_rows2 = flip(own_rows, "c")
    kv = keys_values(own_rows, own_rows2)
    query = project(every, states, 0, tie(wq, wo, *kv), hidden.shape[1], span, True)
    attn, prob = attend(0, at, query, kv, span, head_dim)
    other_rows = jnp.concatenate(lax.optimization_barrier((*other_rows, attn))[:-1], axis=0)
    other_rows2 = flip(other_rows, "c")
    hop_out = tie(hop_out, query)
    hop_out_x = flip(hop_out, "x")
    kv2 = keys_values(other_rows, other_rows2)
    attn2, prob2 = attend(1, at, query, kv2, span, head_dim)
    some = project(at_of(out_pieces), states, 1, tie(wo, attn2), rows_here, span, False)

    late = []
    for hop in range(1, nzh):
        if hop > 1:
            hop_out = onward(hop_out, "zh")
            hop_out_x = flip(hop_out, "x")
        for at_x, block in ((x, hop_out), (1 - x, hop_out_x)):
            late.append((shard_at(hop, zl, at_x), block, 0, rows_here, None))
            late.append((shard_at(hop, 1 - zl, at_x), block, rows_here, rows_here, None))

    hop_out_x = tie(hop_out_x, some)
    late[-2:] = [(p[0], hop_out_x) + p[2:] for p in late[-2:]]
    wo = place(late, w_dims, wo)
    attn = (attn, attn2)
    out_sent = core_sums(attn, wo)
    if out_sent is not None:
        some = tie(some, out_sent)
    d_attn = project(at_of(late), states, 1, wo, rows_here, span, True, some)
    cca_out, moved, arrived = sum_heads((attn[0], tie(attn[1], d_attn)), wo, out_sent)
    d_attn = tie(d_attn, *moved)
    *d_query, grad_sent = backward((prob, prob2), d_attn, (kv, kv2), wq, span, head_dim)
    if arrived:
        grad_sent = tie(grad_sent, *arrived[1:])
    hidden_grad, _, _ = sum_heads(d_query, wq, grad_sent)
    return (cca_out, hidden_grad)


def solution(mesh):
    ns, nm = mesh.shape["seq"], mesh.shape["mp"]
    fine = Mesh(mesh.devices.reshape(ns // 4, 2, 2, nm // 2, 2), ("zh", "zl", "x", "y", "c"))
    seq, mp = SEQ, ("y", "c")
    return jax.shard_map(
        per_device,
        mesh=fine,
        in_specs=(
            P(seq, mp),
            P(seq, mp),
            P(seq, None, None),
            P(),
            P(mp, None),
            P(mp, None),
            P(mp, None),
            P(seq, mp, None),
            P(seq, mp, None, None),
            P(seq, mp, None),
        ),
        out_specs=(P(seq, mp), P(seq, mp)),
        check_vma=False,
    )
```
